128 devices in a mesh: dp: 32 (over y, x, core), head: 4 (over z).
Axes of the slice: x: 4, y: 4, z: 4, core: 2. Of those that a mesh axis runs over, the one named last changes fastest.
Arguments:
- tile_features: bfloat16 [64, 1601, 7680], P('dp', None, 'head'), may hold values from -6 to 6
- projection: bfloat16 [7680, 8, 256], P('head'), may hold values from -0.09375 to 0.09375
- queries: bfloat16 [32, 64, 8192], P('dp', None, 'head'), may hold values from -36 to 36
- query_gain: float32 [128], replicated, may hold values from 1 to 2.2
- key_gain: float32 [128], replicated, may hold values from 1 to 2.2
- tile_count: int32 [32], P('dp'), may hold values from 1 to 4, as said below
- tile_slot: int32 [32, 4], P('dp'), may hold values from 0 to 63, as said below
- cross_mask: int32 [32, 64, 4], P('dp'), may hold values 0 or 1
- prompt_length: int32 [32], P('dp'), may hold values from 16 to 64, as said below
Outputs:
- context: bfloat16 [32, 64, 8192], P('dp', None, 'head')
The draws below stay inside these ranges and needn't reach their ends.
Inputs may be any that keep to these rules, and one draw needn't show every extreme that they name: `tile_count`: the counts of each aligned group of 4 requests sum to 8; some request has 4 tiles and some has one. Slot s sits on index s // 2 of dp; every slot holds exactly one tile; for t < tile_count[r], tile_slot[r, t] is the slot of tile t of request r, one of the 8 slots of the aligned group of 4 indices of dp that holds request r; entries with t >= tile_count[r] are arbitrary slots. `prompt_length`: some request uses all 64 rows.
All inputs are finite; a program needn't handle non-finite values. No bound on the sum of `cross_mask` on one device may be relied on, other than what follows from the above.
Results may differ from the reference program's by a relative error of at most 0.04.
Values may be sent and summed in bfloat16 or wider, within the bound.
No kernel may reach another device: no remote copies, remote signals or barrier semaphores. Data moves between devices by JAX's collectives and lax.ppermute only.
A program may use at most 128 MiB of HBM per device.

```python
import math
import jax
import jax.numpy as jnp
import numpy as np
from jax import lax

VDIM = 7680
HEADS = 64
KVH = 8
HD = 128
TROWS = 1601
MAXT = 4
TILES_DEV = 2
GROUP = 4
PROMPT = 64
REQUESTS = 32
SLOTS = 64
N_HEAD = 4


def count_rows():
    combos = np.arange(MAXT ** GROUP)
    powers = MAXT ** np.arange(GROUP)
    grid = combos[:, None] // powers[None, :] % MAXT + 1
    kept_rows = grid[grid.sum(axis=1) == GROUP * TILES_DEV]
    return jnp.asarray(kept_rows, dtype=jnp.int32)


def tile_layout(key):
    groups = REQUESTS // GROUP
    group_slots = GROUP * TILES_DEV
    table = count_rows()
    chosen = jax.random.randint(jax.random.fold_in(key, 11), (groups,), 0, table.shape[0])
    counts = table[chosen]
    forced_group = jax.random.randint(jax.random.fold_in(key, 12), (), 0, groups)
    forced = jax.random.permutation(jax.random.fold_in(key, 13), jnp.array([MAXT, 1, 1, group_slots - MAXT - 2], dtype=jnp.int32))
    counts = jnp.where((jnp.arange(groups) == forced_group)[:, None], forced[None, :], counts)
    shuffle_keys = jax.random.split(jax.random.fold_in(key, 14), groups)
    shuffles = jax.vmap(lambda one_key: jax.random.permutation(one_key, group_slots))(shuffle_keys).astype(jnp.int32)
    starts = jnp.cumsum(counts, axis=1) - counts
    tile_range = jnp.arange(MAXT, dtype=jnp.int32)
    positions = jnp.minimum(starts[:, :, None] + tile_range[None, None, :], group_slots - 1)
    picked = jnp.take_along_axis(shuffles, positions.reshape(groups, GROUP * MAXT), axis=1).reshape(groups, GROUP, MAXT)
    slots = picked + (jnp.arange(groups, dtype=jnp.int32) * group_slots)[:, None, None]
    usable = tile_range[None, None, :] < counts[:, :, None]
    filler = jax.random.randint(jax.random.fold_in(key, 15), (groups, GROUP, MAXT), 0, SLOTS)
    tile_slot = jnp.where(usable, slots, filler).reshape(REQUESTS, MAXT).astype(jnp.int32)
    return (counts.reshape(REQUESTS).astype(jnp.int32), tile_slot)


def draw_tile_count(key, part):
    counts, slots = tile_layout(key)
    return counts


def draw_tile_slot(key, part):
    counts, slots = tile_layout(key)
    return slots


def draw_prompt_length(key, part):
    key = jax.random.fold_in(key, 3)
    lengths = jax.random.randint(jax.random.fold_in(key, 1), (REQUESTS,), PROMPT // 4, PROMPT + 1)
    full_index = jax.random.randint(jax.random.fold_in(key, 2), (), 0, REQUESTS)
    return jnp.where(jnp.arange(REQUESTS) == full_index, PROMPT, lengths).astype(jnp.int32)


def draw_queries(key, part):
    key = jax.random.fold_in(key, 4)
    shape = (REQUESTS, PROMPT, HEADS * HD)
    row_scale = jnp.exp(jax.random.uniform(jax.random.fold_in(key, 1), (REQUESTS, PROMPT, 1), minval=math.log(0.3), maxval=math.log(3.0)))
    column_scale = jnp.exp(jax.random.uniform(jax.random.fold_in(key, 2), (1, 1, HEADS * HD), minval=math.log(0.3), maxval=math.log(3.0)))
    normal_part = jnp.clip(jax.random.normal(jax.random.fold_in(key, 3), shape), -4.0, 4.0)
    return (normal_part * row_scale * column_scale).astype(jnp.bfloat16)


def with_ends(entries, stream_key, least, high):
    index_at = [jax.random.randint(jax.random.fold_in(stream_key, axis), (), 0, length) for axis, length in enumerate(entries.shape)]
    widest = entries.shape.index(max(entries.shape))
    beside = index_at[:widest] + [(index_at[widest] + 1) % entries.shape[widest]] + index_at[widest + 1:]
    return entries.at[tuple(index_at)].set(least).at[tuple(beside)].set(high)


def raised(values, stream_key, source, target, parts, factor):
    def block_of(axis_at):
        return (jnp.arange(values.shape[axis_at]) // (values.shape[axis_at] // parts)).reshape((-1,) + (1,) * (values.ndim - 1 - axis_at))

    first = jax.random.permutation(stream_key, parts)[block_of(target)]
    other_side = (block_of(target) + parts // 2) % parts
    return jnp.where((block_of(source) == first) | (block_of(source) == other_side), factor * values, values)


def block_levels(key, dims, shards, low, largest):
    factor_of = 1.0
    for dim, blocks in shards:
        draws = jax.random.uniform(jax.random.fold_in(jax.random.fold_in(key, 6), dim), (blocks,), jnp.float32, low / len(shards), largest / len(shards))
        factor_of = factor_of * jnp.repeat(jnp.exp(draws), dims[dim] // blocks).reshape((-1,) + (1,) * (len(dims) - 1 - dim))
    return factor_of


def scatter_about(own_key, shape, spread, most, cuts=(), held_as=jnp.bfloat16):
    values = jax.random.normal(own_key, shape, jnp.float32) * spread
    if len(cuts) > 0:
        values = block_levels(own_key, shape, cuts, -0.22, 0.18) * values
    return jnp.clip(values, min=-most, max=most).astype(held_as)


def gaussian_with(key, dims, width, reach, shards, heavy, held_as=jnp.bfloat16):
    values = width * jax.random.normal(key, dims, jnp.float32)
    if shards:
        values = values * block_levels(key, dims, shards, -0.22, 0.18)
    return jnp.clip(raised(values, jax.random.fold_in(key, 3), *heavy), -reach, reach).astype(held_as)


def setup_inputs(seed: int = 0) -> dict:
    streams_of = jax.random.split(jax.random.key(seed), 10)
    return {
        "tile_features": scatter_about(streams_of[0], (SLOTS, TROWS, VDIM), 1.0, 6.0, ((0, 32), (2, 4))),
        "projection": gaussian_with(streams_of[1], (VDIM, KVH, 2 * HD), VDIM ** -0.5, 0.09375, ((0, 4),), (0, 1, 4, 2.0)),
        "queries": draw_queries(jax.random.fold_in(streams_of[9], 71), 0),
        "query_gain": jnp.clip(jnp.exp(jax.random.uniform(streams_of[3], (HD,), jnp.float32, math.log(1.0), math.log(2.2))), 1.0, 2.2),
        "key_gain": jnp.clip(jnp.exp(jax.random.uniform(streams_of[4], (HD,), jnp.float32, math.log(1.0), math.log(2.2))), 1.0, 2.2),
        "tile_count": draw_tile_count(jax.random.fold_in(streams_of[9], 71), 0),
        "tile_slot": draw_tile_slot(jax.random.fold_in(streams_of[9], 71), 0),
        "cross_mask": with_ends((jax.random.randint(streams_of[7], (REQUESTS, PROMPT, MAXT), 0, 4) < 3).astype(jnp.int32), jax.random.fold_in(streams_of[7], 1), 0, 1),
        "prompt_length": draw_prompt_length(jax.random.fold_in(streams_of[9], 71), 0),
    }


def round_half(values):
    return lax.optimization_barrier(values.astype(jnp.bfloat16))

def normalize_rows(values, row_gain):
    squares = lax.optimization_barrier(jnp.mean(values * values, axis=-1, keepdims=True))
    return values * lax.rsqrt(squares + 1e-05) * row_gain

def reference(tile_features, projection, queries, query_gain, key_gain, tile_count, tile_slot, cross_mask, prompt_length):
    group_width = VDIM // N_HEAD
    group_size = HEADS // KVH
    flat_rows = tile_features.reshape(SLOTS * TROWS, VDIM)
    flat_weight = projection.reshape(VDIM, KVH * 2 * HD)

    def add_group(group_index, running):
        first_column = (group_index * group_width).astype(jnp.int32)
        columns = lax.dynamic_slice_in_dim(flat_rows, first_column, group_width, 1)
        weight_rows = lax.dynamic_slice_in_dim(flat_weight, first_column, group_width, 0)
        partial_value = jnp.dot(columns, weight_rows, preferred_element_type=jnp.float32)
        return running + round_half(partial_value).astype(jnp.float32)
    running = lax.fori_loop(0, N_HEAD, add_group, jnp.zeros((SLOTS * TROWS, KVH * 2 * HD), jnp.float32))
    kv_tiles = round_half(running).reshape(SLOTS, TROWS, KVH, 2 * HD)
    keys_normed = round_half(normalize_rows(kv_tiles[..., :HD].astype(jnp.float32), key_gain))
    tile_values = kv_tiles[..., HD:]
    query_heads = queries.reshape(REQUESTS, PROMPT, KVH, group_size, HD)
    queries_normed = round_half(normalize_rows(query_heads.astype(jnp.float32), query_gain))
    score_scale = 1.0 / math.sqrt(HD)
    row_index = jnp.arange(PROMPT, dtype=jnp.int32)
    tile_range = jnp.arange(MAXT, dtype=jnp.int32)

    def attend(inputs):
        query_block, own_count, own_slots, own_mask, own_length = inputs
        numerator = jnp.zeros((PROMPT, KVH, group_size, HD), jnp.float32)
        denominator = jnp.zeros((PROMPT, KVH, group_size), jnp.float32)
        for tile_pos in range(MAXT):
            slot_here = own_slots[tile_pos].astype(jnp.int32)
            key_tile = lax.dynamic_index_in_dim(keys_normed, slot_here, 0, keepdims=False)
            value_tile = lax.dynamic_index_in_dim(tile_values, slot_here, 0, keepdims=False)
            scores = jnp.einsum('pkgd,nkd->pkgn', query_block.astype(jnp.float32), key_tile.astype(jnp.float32)) * score_scale
            usable = (own_mask[:, tile_pos] == 1) & (tile_pos < own_count) & (row_index < own_length)
            weights = round_half(jnp.where(usable[:, None, None, None], jnp.exp(scores), 0.0)).astype(jnp.float32)
            denominator = denominator + lax.optimization_barrier(jnp.sum(weights, axis=-1))
            numerator = numerator + jnp.einsum('pkgn,nkd->pkgd', weights, value_tile.astype(jnp.float32))
        live_rows = (row_index < own_length) & jnp.any((own_mask == 1) & (tile_range[None, :] < own_count), axis=1)
        divisor = jnp.where(live_rows[:, None, None], denominator, 1.0)
        result = jnp.where(live_rows[:, None, None, None], numerator / divisor[..., None], 0.0)
        return result.reshape(PROMPT, HEADS * HD).astype(jnp.bfloat16)
    return lax.map(attend, (queries_normed, tile_count, tile_slot, cross_mask, prompt_length))
```

```python
import math

import jax
import jax.numpy as jnp
from jax import lax
from jax.experimental import pallas as pl
from jax.experimental.pallas import tpu as pltpu
from jax.sharding import PartitionSpec as P

KVH = 8
HD = 128
MAXT = 4
GROUP = 4
NHEAD = 4
GSIZE = 8
PROMPT = 64
QROWS = GSIZE * PROMPT
TROWS = 1601
WIDTH = 1920
TILES = 2
HEADS_HERE = 2
HALF = 808
SMALL = 280
LARGE = HALF - SMALL
UP_SMALL, UP_LARGE = 0, SMALL
DOWN_LARGE, DOWN_SMALL = TROWS - HALF, TROWS - SMALL
OVERLAP = 2 * HALF - TROWS
SENT_ROWS = QROWS + 16
F32 = jnp.float32
BF16 = jnp.bfloat16
VMEM_LIMIT = 56 * 2**20


def params():
    return pltpu.CompilerParams(vmem_limit_bytes=VMEM_LIMIT)


def cost(flops, moved, exps=0):
    return pl.CostEstimate(flops=flops, bytes_accessed=moved, transcendentals=exps)


def split_heads_kernel(w_ref, out_ref):
    out_ref[...] = jnp.transpose(w_ref[...], (1, 0, 2))


def split_heads(projection):
    depth = 480
    return pl.pallas_call(
        split_heads_kernel,
        grid=(WIDTH // depth,),
        in_specs=[pl.BlockSpec((depth, KVH, 2 * HD), lambda i: (i, 0, 0))],
        out_specs=pl.BlockSpec((KVH, depth, 2 * HD), lambda i: (0, i, 0)),
        out_shape=jax.ShapeDtypeStruct((KVH, WIDTH, 2 * HD), BF16),
        compiler_params=params(),
        cost_estimate=cost(0, 4 * WIDTH * KVH * HD * 2),
        name="split_heads",
    )(projection)


def first_partial_kernel(shard_ref, x_ref, w_ref, low_ref, high_ref, flat_ref):
    rows = x_ref.shape[0]
    flat = x_ref[...].reshape(2 * rows, WIDTH)
    flat_ref[...] = flat
    low_ref[...] = jnp.dot(flat, w_ref[0], preferred_element_type=F32).astype(BF16)
    high_ref[...] = jnp.dot(flat, w_ref[1], preferred_element_type=F32).astype(BF16)


def first_partial(shards, rows_first, weights, start, count, blocks):
    block = count // blocks
    return pl.pallas_call(
        first_partial_kernel,
        grid_spec=pltpu.PrefetchScalarGridSpec(
            num_scalar_prefetch=1,
            grid=(blocks,),
            in_specs=[
                pl.BlockSpec(
                    (pl.Element(block), pl.Element(TILES), pl.Element(WIDTH)),
                    lambda i, s: (start + i * block, 0, 0),
                ),
                pl.BlockSpec((HEADS_HERE, WIDTH, 2 * HD), lambda i, s: (s[0], 0, 0)),
            ],
            out_specs=[
                pl.BlockSpec((2 * block, 2 * HD), lambda i, s: (i, 0)),
                pl.BlockSpec((2 * block, 2 * HD), lambda i, s: (i, 0)),
                pl.BlockSpec((2 * block, WIDTH), lambda i, s: (i, 0)),
            ],
        ),
        out_shape=[
            jax.ShapeDtypeStruct((2 * count, 2 * HD), BF16),
            jax.ShapeDtypeStruct((2 * count, 2 * HD), BF16),
            jax.ShapeDtypeStruct((2 * count, WIDTH), BF16),
        ],
        compiler_params=params(),
        cost_estimate=cost(2 * 2 * count * WIDTH * 512, 2 * count * WIDTH * 4),
        name="first_partial",
    )(shards, rows_first, weights)


def later_partials_kernel(shard_ref, flat_ref, w_ref, *out_refs):
    step = pl.program_id(0)
    low = jnp.dot(flat_ref[...], w_ref[0], preferred_element_type=F32).astype(BF16)
    high = jnp.dot(flat_ref[...], w_ref[1], preferred_element_type=F32).astype(BF16)
    for at in range(NHEAD - 1):

        @pl.when(step == at)
        def _():
            out_refs[2 * at][...] = low
            out_refs[2 * at + 1][...] = high


def later_partials(shards, flat, weights):
    rows = flat.shape[0]
    outs = 2 * (NHEAD - 1)
    return pl.pallas_call(
        later_partials_kernel,
        grid_spec=pltpu.PrefetchScalarGridSpec(
            num_scalar_prefetch=1,
            grid=(NHEAD - 1,),
            in_specs=[
                pl.BlockSpec((rows, WIDTH), lambda i, s: (0, 0)),
                pl.BlockSpec((HEADS_HERE, WIDTH, 2 * HD), lambda i, s: (s[i + 1], 0, 0)),
            ],
            out_specs=[pl.BlockSpec((rows, 2 * HD), lambda i, s: (0, 0))] * outs,
        ),
        out_shape=[jax.ShapeDtypeStruct((rows, 2 * HD), BF16)] * outs,
        compiler_params=params(),
        cost_estimate=cost(3 * 2 * rows * WIDTH * 512, rows * WIDTH * 2),
        name="later_partials",
    )(shards, flat, weights)


def query_kernel(info_ref, mask_ref, q_ref, gain_ref, qn_ref, owned_ref):
    me = info_ref[GROUP, 0]
    own = lax.rem(me, GROUP)
    for tile in range(TILES):
        slot = me * TILES + tile
        asker = jnp.int32(0)
        place = jnp.int32(0)
        for request in range(GROUP):
            for at in range(MAXT):
                hit = (info_ref[request, 2 + at] == slot) & (at < info_ref[request, 0])
                asker = jnp.where(hit, request, asker)
                place = jnp.where(hit, at, place)
        length = info_ref[asker, 1]
        lane = lax.broadcasted_iota(jnp.int32, (PROMPT, MAXT), 1)
        seen = jnp.sum(jnp.where(lane == place, mask_ref[asker], 0), axis=1, keepdims=True)
        row = lax.broadcasted_iota(jnp.int32, (PROMPT, HD), 0)
        usable = (jnp.broadcast_to(seen, (PROMPT, HD)) == 1) & (row < length)
        for partner in range(GROUP):
            mine = lax.bitwise_xor(own, partner) == asker
            owned_ref[partner, tile] = jnp.where(usable & mine, 1.0, 0.0)
        for head in range(HEADS_HERE):
            for member in range(GSIZE):
                column = (head * GSIZE + member) * HD
                values = q_ref[asker, :, column : column + HD].astype(F32)
                squares = jnp.mean(values * values, axis=-1, keepdims=True)
                normed = values * lax.rsqrt(squares + 1e-05) * gain_ref[...]
                qn_ref[head, tile, member * PROMPT : (member + 1) * PROMPT, :] = normed.astype(BF16)


def prepare_queries(info, masks, queries, query_gain):
    vmem = pl.BlockSpec(memory_space=pltpu.VMEM)
    return pl.pallas_call(
        query_kernel,
        in_specs=[pl.BlockSpec(memory_space=pltpu.SMEM), vmem, vmem, vmem],
        out_specs=[vmem, vmem],
        out_shape=[
            jax.ShapeDtypeStruct((HEADS_HERE, TILES, QROWS, HD), BF16),
            jax.ShapeDtypeStruct((GROUP, TILES, PROMPT, HD), F32),
        ],
        compiler_params=params(),
        cost_estimate=cost(2**22, 2**21),
        name="prepare_queries",
    )(info, masks, queries, query_gain)


def attend(up, up_own, down, down_own, qn_ref, gain_ref, total_ref, scratch, skip, first):
    key_scr, value_scr = scratch
    for part, (got, own) in enumerate(((up, up_own), (down, down_own))):
        rows = got.shape[0] // 2
        both = (got[...].astype(F32) + own[...].astype(F32)).astype(BF16).astype(F32)
        key_scr[...] = both[:, :HD]
        value_scr[...] = both[:, HD:]
        for tile in range(TILES):
            keys = key_scr[pl.ds(tile, rows, stride=2), :]
            values = value_scr[pl.ds(tile, rows, stride=2), :]
            squares = jnp.mean(keys * keys, axis=-1, keepdims=True)
            keys = (keys * lax.rsqrt(squares + 1e-05) * gain_ref[...]).astype(BF16)
            ones = jnp.ones((rows, HD), F32)
            if part == 1 and skip:
                keep = lax.broadcasted_iota(jnp.int32, (rows, HD), 0) >= skip
                values = jnp.where(keep, values, 0.0)
                ones = jnp.where(keep, 1.0, 0.0)
            wide = jnp.concatenate([values, ones], axis=1).astype(BF16)
            scores = lax.dot_general(
                qn_ref[0, tile], keys, (((1,), (1,)), ((), ())), preferred_element_type=F32
            )
            weights = jnp.exp(scores * (1.0 / math.sqrt(HD))).astype(BF16)
            term = jnp.dot(weights, wide, preferred_element_type=F32)
            if first and part == 0:
                total_ref[tile] = term
            else:
                total_ref[tile] += term


def partial_attention(head, parts, qn, key_gain, skip):
    rows = parts[0].shape[0]

    def body(up, up_own, down, down_own, qn_ref, gain_ref, total_ref, *scratch):
        attend(up, up_own, down, down_own, qn_ref, gain_ref, total_ref, scratch, skip, True)

    return pl.pallas_call(
        body,
        grid=(1,),
        in_specs=[pl.BlockSpec((rows, 2 * HD), lambda i: (0, 0))] * 4
        + [
            pl.BlockSpec((1, TILES, QROWS, HD), lambda i: (head, 0, 0, 0)),
            pl.BlockSpec((1, HD), lambda i: (0, 0)),
        ],
        out_specs=pl.BlockSpec((TILES, QROWS, 2 * HD), lambda i: (0, 0, 0)),
        out_shape=jax.ShapeDtypeStruct((TILES, QROWS, 2 * HD), F32),
        scratch_shapes=[pltpu.VMEM((rows, HD), F32)] * 2,
        compiler_params=params(),
        cost_estimate=cost(2 * 2 * rows * QROWS * 384, rows * 2048, 2 * rows * QROWS),
        name="partial_attention",
    )(*parts, qn, key_gain)


def diagonal(shape):
    row = lax.broadcasted_iota(jnp.int32, shape, 0)
    column = lax.broadcasted_iota(jnp.int32, shape, 1)
    return jnp.where(row == column, 1.0, 0.0).astype(F32)


def closing_attention(head, parts, qn, key_gain, before, owned, skip):
    rows = parts[0].shape[0]

    def body(
        up, up_own, down, down_own, qn_ref, gain_ref, before_ref, owned_ref, kept, *rest
    ):
        sent, (total_ref, key_scr, value_scr) = rest[: GROUP - 1], rest[GROUP - 1 :]
        total_ref[...] = before_ref[...]
        scratch = (key_scr, value_scr)
        attend(up, up_own, down, down_own, qn_ref, gain_ref, total_ref, scratch, skip, False)
        eye = diagonal((HD, HD))
        for partner in range(GROUP):
            rows_of = []
            for member in range(GSIZE):
                block = slice(member * PROMPT, (member + 1) * PROMPT)
                for part in range(2):
                    lanes = slice(part * HD, (part + 1) * HD)
                    held = jnp.zeros((PROMPT, HD), F32)
                    for tile in range(TILES):
                        belongs = owned_ref[partner, tile] > 0.5
                        held += jnp.where(belongs, total_ref[tile, block, lanes], 0.0)
                    if partner == 0:
                        kept[block, lanes] = held
                    elif part == 0:
                        sent[partner - 1][block, :] = held.astype(BF16)
                    else:
                        rows_of.append(held)
            if partner == 0:
                continue
            lines = []
            for at in range(QROWS // HD):
                square = jnp.concatenate([rows_of[2 * at], rows_of[2 * at + 1]], axis=0)
                lines.append(jnp.sum(square * eye, axis=0, keepdims=True))
            lines = jnp.concatenate(lines, axis=0)
            coarse = lines.astype(BF16).astype(F32)
            tail = jnp.concatenate([coarse, lines - coarse, jnp.zeros((8, HD), F32)], axis=0)
            sent[partner - 1][QROWS:, :] = tail.astype(BF16)

    whole = lambda *shape: pl.BlockSpec(shape, lambda i: (0,) * len(shape))
    return pl.pallas_call(
        body,
        grid=(1,),
        in_specs=[whole(rows, 2 * HD)] * 4
        + [
            pl.BlockSpec((1, TILES, QROWS, HD), lambda i: (head, 0, 0, 0)),
            whole(1, HD),
            whole(TILES, QROWS, 2 * HD),
            whole(GROUP, TILES, PROMPT, HD),
        ],
        out_specs=[whole(QROWS, 2 * HD)] + [whole(SENT_ROWS, HD)] * (GROUP - 1),
        out_shape=[jax.ShapeDtypeStruct((QROWS, 2 * HD), F32)]
        + [jax.ShapeDtypeStruct((SENT_ROWS, HD), BF16)] * (GROUP - 1),
        scratch_shapes=[pltpu.VMEM((TILES, QROWS, 2 * HD), F32)]
        + [pltpu.VMEM((rows, HD), F32)] * 2,
        compiler_params=params(),
        cost_estimate=cost(2 * 2 * rows * QROWS * 384, rows * 2048, 2 * rows * QROWS),
        name="closing_attention",
    )(*parts, qn, key_gain, before, owned)


def finish_kernel(info_ref, mask_ref, *refs):
    out_ref = refs[-1]
    lane = lax.broadcasted_iota(jnp.int32, (PROMPT, MAXT), 1)
    seen = jnp.where((lane < info_ref[0, 0]) & (mask_ref[0] == 1), 1, 0)
    seen = jnp.sum(seen, axis=1, keepdims=True)
    row = lax.broadcasted_iota(jnp.int32, (PROMPT, HD), 0)
    live = (jnp.broadcast_to(seen, (PROMPT, HD)) > 0) & (row < info_ref[0, 1])
    eye = diagonal((HD, HD))
    for head in range(HEADS_HERE):
        kept, *got = refs[head * GROUP : (head + 1) * GROUP]
        for at in range(QROWS // HD):
            line = jnp.zeros((1, HD), F32)
            for one in got:
                line += one[QROWS + at : QROWS + at + 1, :].astype(F32)
                line += one[QROWS + 4 + at : QROWS + 5 + at, :].astype(F32)
            square = jnp.broadcast_to(line, (HD, HD)) * eye
            spread = jnp.broadcast_to(jnp.sum(square, axis=1, keepdims=True), (HD, HD))
            block = slice(at * HD, (at + 1) * HD)
            numerator = kept[block, :HD]
            for one in got:
                numerator += one[block, :].astype(F32)
            denominator = kept[block, HD:] + spread
            for half in range(HD // PROMPT):
                inner = slice(half * PROMPT, (half + 1) * PROMPT)
                divisor = jnp.where(live, denominator[inner], 1.0)
                result = jnp.where(live, numerator[inner] / divisor, 0.0)
                column = (head * GSIZE + at * 2 + half) * HD
                out_ref[0, :, column : column + HD] = result.astype(BF16)


def finish(info, mask, parts):
    vmem = pl.BlockSpec(memory_space=pltpu.VMEM)
    return pl.pallas_call(
        finish_kernel,
        in_specs=[pl.BlockSpec(memory_space=pltpu.SMEM)] + [vmem] * (1 + len(parts)),
        out_specs=vmem,
        out_shape=jax.ShapeDtypeStruct((1, PROMPT, HEADS_HERE * GSIZE * HD), BF16),
        compiler_params=params(),
        cost_estimate=cost(2**21, 2**21),
        name="finish",
    )(info, mask, *parts)


def add(left, right):
    return (left.astype(F32) + right.astype(F32)).astype(BF16)


def local(
    tile_features,
    projection,
    queries,
    query_gain,
    key_gain,
    tile_count,
    tile_slot,
    cross_mask,
    prompt_length,
):
    here = lax.axis_index("head")
    own_index = lax.axis_index("dp")
    steps = jnp.arange(1, NHEAD + 1, dtype=jnp.int32)
    up_shards = lax.rem(here - steps + 2 * NHEAD, NHEAD)
    down_shards = lax.rem(here + steps, NHEAD)
    up_perm = [(i, (i + 1) % NHEAD) for i in range(NHEAD)]
    down_perm = [(i, (i - 1) % NHEAD) for i in range(NHEAD)]
    groups = [list(range(g, g + GROUP)) for g in range(0, lax.axis_size("dp"), GROUP)]

    weights = split_heads(projection)
    rows_first = jnp.transpose(tile_features, (1, 0, 2))
    plan = {
        "us": (up_shards, up_perm, UP_SMALL, SMALL, 1),
        "ds": (down_shards, down_perm, DOWN_SMALL, SMALL, 1),
        "ul": (up_shards, up_perm, UP_LARGE, LARGE, 2),
        "dl": (down_shards, down_perm, DOWN_LARGE, LARGE, 2),
    }
    running, flats, owned_parts = {}, {}, {}
    for name, (shards, perm, start, count, blocks) in plan.items():
        low, high, flat = first_partial(shards, rows_first, weights, start, count, blocks)
        running[name, 0], running[name, 1] = low, high
        flats[name] = flat
    for name, (shards, perm, start, count, blocks) in plan.items():
        outs = later_partials(shards, flats[name], weights)
        for at in range(NHEAD - 1):
            owned_parts[name, 0, at] = outs[2 * at]
            owned_parts[name, 1, at] = outs[2 * at + 1]
    order = [("us", 0), ("ds", 0), ("us", 1), ("ds", 1), ("ul", 0), ("dl", 0), ("ul", 1), ("dl", 1)]
    for step in range(NHEAD - 1):
        for name, head in order:
            got = lax.ppermute(running[name, head], "head", plan[name][1])
            if step < NHEAD - 2:
                got = add(got, owned_parts[name, head, step])
            running[name, head] = got

    info = jnp.concatenate([tile_count, prompt_length, tile_slot[0], jnp.zeros((2,), jnp.int32)])
    packed = jnp.concatenate([info, cross_mask.reshape(-1)])[None]
    packed_all = lax.all_gather(packed, "dp", axis=0, tiled=True, axis_index_groups=groups)
    queries_all = lax.all_gather(queries, "dp", axis=0, tiled=True, axis_index_groups=groups)
    last_line = jnp.full((1, 8), own_index, jnp.int32)
    info_all = jnp.concatenate([packed_all[:, :8], last_line], axis=0)
    masks_all = packed_all[:, 8:].reshape(GROUP, PROMPT, MAXT)
    qn, owned = prepare_queries(info_all, masks_all, queries_all, query_gain[None])

    key_line = key_gain[None]
    final = []
    last = NHEAD - 2
    for head in range(HEADS_HERE):

        def parts_of(up, down):
            return (
                running[up, head],
                owned_parts[up, head, last],
                running[down, head],
                owned_parts[down, head, last],
            )

        before = partial_attention(head, parts_of("us", "ds"), qn, key_line, 0)
        kept, *sent = closing_attention(
            head, parts_of("ul", "dl"), qn, key_line, before, owned, OVERLAP
        )
        final.append(kept)
        for partner in range(1, GROUP):
            pairs = [(i, i ^ partner) for i in range(lax.axis_size("dp"))]
            final.append(lax.ppermute(sent[partner - 1], "dp", pairs))
    return finish(info[None], cross_mask, final)


def solution(mesh):
    in_specs = (
        P("dp", None, "head"),
        P("head", None, None),
        P("dp", None, "head"),
        P(),
        P(),
        P("dp"),
        P("dp", None),
        P("dp", None, None),
        P("dp"),
    )
    out_specs = P("dp", None, "head")
    return jax.shard_map(local, mesh=mesh, in_specs=in_specs, out_specs=out_specs, check_vma=False)
```

```python
import math

import jax
import jax.numpy as jnp
from jax import lax
from jax.experimental import pallas as pl
from jax.experimental.pallas import tpu as pltpu
from jax.sharding import PartitionSpec as P

KVH = 8
HD = 128
MAXT = 4
GROUP = 4
NHEAD = 4
GSIZE = 8
PROMPT = 64
QROWS = GSIZE * PROMPT
TROWS = 1601
WIDTH = 1920
TILES = 2
HEADS_HERE = 2
HALF = 808
FRONT = 448
BACK = HALF - FRONT
UP_FRONT, UP_BACK = 0, FRONT
DOWN_BACK, DOWN_FRONT = TROWS - HALF, TROWS - FRONT
OVERLAP = 2 * HALF - TROWS
SENT_ROWS = QROWS + 16
F32 = jnp.float32
BF16 = jnp.bfloat16
VMEM_LIMIT = 56 * 2**20
PAIR = 4 * HD
CUTS = (0, 768, 1536, WIDTH)


def params():
    return pltpu.CompilerParams(vmem_limit_bytes=VMEM_LIMIT)


def brief():
    return pl.CostEstimate(flops=2**10, bytes_accessed=2**10, transcendentals=0)


def lasting():
    return pl.CostEstimate(flops=10**11, bytes_accessed=2**24, transcendentals=0)


def shard_at(side, step):
    here = lax.axis_index("head")
    return lax.rem(here + (NHEAD - step if side == 0 else step), NHEAD)


def open_ring_kernel(w_hbm, x_hbm, *refs):
    outs, wt_hbm = refs[:4], refs[4]
    raw, turned, held, totals, raw_sem, out_sem, x_sem = refs[5:]

    def raw_copy(at):
        depth = pl.ds(CUTS[at], CUTS[at + 1] - CUTS[at])
        return pltpu.make_async_copy(w_hbm.at[depth], raw.at[depth], raw_sem.at[at])

    def turned_copy(at):
        depth = pl.ds(CUTS[at], CUTS[at + 1] - CUTS[at])
        return pltpu.make_async_copy(turned.at[:, depth], wt_hbm.at[:, depth], out_sem.at[at])

    def row_copy(side):
        start = (UP_FRONT, DOWN_FRONT)[side]
        return pltpu.make_async_copy(x_hbm.at[pl.ds(start, FRONT)], held.at[side], x_sem.at[side])

    chunks = len(CUTS) - 1
    row_copy(0).start()
    raw_copy(0).start()
    row_copy(1).start()
    for at in range(1, chunks):
        raw_copy(at).start()
    shards = [shard_at(side, 1) for side in range(2)]
    for at in range(chunks):
        low, high = CUTS[at], CUTS[at + 1]
        raw_copy(at).wait()
        lines = jnp.transpose(raw[low:high], (1, 0, 2))
        for head in range(KVH):
            lanes = slice(head % 2 * 2 * HD, (head % 2 + 1) * 2 * HD)
            turned[head // 2, low:high, lanes] = lines[head]
        turned_copy(at).start()
        for side in range(2):
            if at == 0:
                row_copy(side).wait()
            flat = held[side, :, :, low:high].reshape(2 * FRONT, high - low)
            term = jnp.dot(flat, turned[shards[side], low:high], preferred_element_type=F32)
            if at > 0:
                term = totals[side] + term
            if at < chunks - 1:
                totals[side] = term
            else:
                outs[2 * side][...] = term[:, : 2 * HD].astype(BF16)
                outs[2 * side + 1][...] = term[:, 2 * HD :].astype(BF16)
    for at in range(chunks):
        turned_copy(at).wait()


def open_ring(projection, rows_first):
    hbm = pl.BlockSpec(memory_space=pl.ANY)
    vmem = pl.BlockSpec(memory_space=pltpu.VMEM)
    chunks = len(CUTS) - 1
    return pl.pallas_call(
        open_ring_kernel,
        in_specs=[hbm, hbm],
        out_specs=[vmem] * 4 + [hbm],
        out_shape=[jax.ShapeDtypeStruct((2 * FRONT, 2 * HD), BF16)] * 4
        + [jax.ShapeDtypeStruct((NHEAD, WIDTH, PAIR), BF16)],
        scratch_shapes=[
            pltpu.VMEM((WIDTH, KVH, 2 * HD), BF16),
            pltpu.VMEM((NHEAD, WIDTH, PAIR), BF16),
            pltpu.VMEM((2, FRONT, TILES, WIDTH), BF16),
            pltpu.VMEM((2, 2 * FRONT, PAIR), F32),
            pltpu.SemaphoreType.DMA((chunks,)),
            pltpu.SemaphoreType.DMA((chunks,)),
            pltpu.SemaphoreType.DMA((2,)),
        ],
        compiler_params=params(),
        cost_estimate=brief(),
        name="open_ring",
    )(projection, rows_first)


def partials_kernel(parts, start, steps, waits, x_hbm, w_hbm, *refs):
    refs = refs[waits:]
    sides = len(parts)
    many = sum(len(part[2]) for part in parts) * steps
    outs, (held, flat, weights, ready, x_sem, w_sem, out_sem) = refs[:many], refs[many:]

    def row_copy(side):
        first, count = parts[side][:2]
        return pltpu.make_async_copy(
            x_hbm.at[pl.ds(first, count)], held.at[side, pl.ds(0, count)], x_sem.at[side]
        )

    def weight_copy(side, step):
        n = side * steps + step
        shard = shard_at(side, start + step)
        return pltpu.make_async_copy(w_hbm.at[shard], weights.at[n], w_sem.at[n])

    for side in range(sides):
        row_copy(side).start()
        for step in range(steps):
            weight_copy(side, step).start()
    copies = []
    for side, (_, count, cuts) in enumerate(parts):
        row_copy(side).wait()
        flat[: 2 * count] = held[side, :count].reshape(2 * count, WIDTH)
        for step in range(steps):
            weight_copy(side, step).wait()
            slot = side * steps + step
            ready[slot, : 2 * count] = jnp.dot(
                flat[: 2 * count], weights[slot], preferred_element_type=F32
            ).astype(BF16)
            for first, size in cuts:
                n = len(copies)
                rows = pl.ds(2 * first, 2 * size)
                copies.append(pltpu.make_async_copy(ready.at[slot, rows], outs[n], out_sem.at[n]))
                copies[-1].start()
    for copy in copies:
        copy.wait()


def partials(rows_first, weights, parts, start, steps, after=()):
    sides = len(parts)
    most = max(part[1] for part in parts)
    sizes = [size for part in parts for _ in range(steps) for first, size in part[2]]
    hbm = pl.BlockSpec(memory_space=pl.ANY)
    return pl.pallas_call(
        lambda *refs: partials_kernel(parts, start, steps, len(after), *refs),
        in_specs=[hbm] * (2 + len(after)),
        out_specs=[hbm] * len(sizes),
        out_shape=[jax.ShapeDtypeStruct((2 * size, PAIR), BF16) for size in sizes],
        scratch_shapes=[
            pltpu.VMEM((sides, most, TILES, WIDTH), BF16),
            pltpu.VMEM((2 * most, WIDTH), BF16),
            pltpu.VMEM((sides * steps, WIDTH, PAIR), BF16),
            pltpu.VMEM((sides * steps, 2 * most, PAIR), BF16),
            pltpu.SemaphoreType.DMA((sides,)),
            pltpu.SemaphoreType.DMA((sides * steps,)),
            pltpu.SemaphoreType.DMA((len(sizes),)),
        ],
        compiler_params=params(),
        cost_estimate=lasting(),
        name="partials",
    )(rows_first, weights, *after)


def join_apart(low, high, own):
    many = len(own)

    def body(*refs):
        for n in range(many):
            for head in range(HEADS_HERE):
                lanes = slice(head * 2 * HD, (head + 1) * 2 * HD)
                total = refs[head * many + n][...].astype(F32)
                total += refs[2 * many + n][:, lanes].astype(F32)
                refs[3 * many + n][:, lanes] = total.astype(BF16)

    vmem = pl.BlockSpec(memory_space=pltpu.VMEM)
    return pl.pallas_call(
        body,
        in_specs=[vmem] * (3 * many),
        out_specs=[vmem] * many,
        out_shape=[jax.ShapeDtypeStruct(one.shape, BF16) for one in own],
        compiler_params=params(),
        cost_estimate=brief(),
        name="join_apart",
    )(*low, *high, *own)


def join_heads(heads, got, own, after, slow):
    many = len(got)
    width = (heads[1] - heads[0]) * 2 * HD

    def body(*refs):
        for n in range(many):
            total = refs[n][...].astype(F32) + refs[many + n][...].astype(F32)
            refs[2 * many + len(after) + n][...] = total.astype(BF16)

    def spec(one, at):
        return pl.BlockSpec((one.shape[0], width), lambda i: (0, at))

    return pl.pallas_call(
        body,
        grid=(1,),
        in_specs=[spec(one, heads[0]) for one in got + own]
        + [pl.BlockSpec(memory_space=pl.ANY)] * len(after),
        out_specs=[spec(one, 0) for one in got],
        out_shape=[jax.ShapeDtypeStruct((one.shape[0], width), BF16) for one in got],
        compiler_params=params(),
        cost_estimate=lasting() if slow else brief(),
        name="join_heads",
    )(*got, *own, *after)


def pack_kernel(info_ref, mask_ref, q_ref, after_ref, out_ref):
    out_ref[0, :, : q_ref.shape[2]] = q_ref[0]
    lane = lax.broadcasted_iota(jnp.int32, (PROMPT, HD), 1)
    words = jnp.zeros((PROMPT, HD), jnp.int32)
    for at in range(MAXT):
        words = jnp.where(lane == at, mask_ref[0, :, at : at + 1], words)
        words = jnp.where(lane == MAXT + at, info_ref[0, 2 + at], words)
    words = jnp.where(lane == 2 * MAXT, info_ref[0, 0], words)
    words = jnp.where(lane == 2 * MAXT + 1, info_ref[0, 1], words)
    out_ref[0, :, q_ref.shape[2] :] = words.astype(F32).astype(BF16)


def pack_queries(info, mask, queries, after):
    vmem = pl.BlockSpec(memory_space=pltpu.VMEM)
    width = queries.shape[2] + HD
    return pl.pallas_call(
        pack_kernel,
        in_specs=[
            pl.BlockSpec(memory_space=pltpu.SMEM),
            vmem,
            vmem,
            pl.BlockSpec(memory_space=pl.ANY),
        ],
        out_specs=vmem,
        out_shape=jax.ShapeDtypeStruct((1, PROMPT, width), BF16),
        compiler_params=params(),
        cost_estimate=brief(),
        name="pack_queries",
    )(info, mask, queries, after)


def query_kernel(me_ref, q_ref, gain_ref, qn_ref, owned_ref):
    me = me_ref[0]
    own = lax.rem(me, GROUP)
    width = q_ref.shape[2] - HD
    lane = lax.broadcasted_iota(jnp.int32, (1, HD), 1)

    def number(request, at):
        line = q_ref[request, 0:16, width:].astype(F32).astype(jnp.int32)[0:1]
        return jnp.sum(jnp.where(lane == at, line, 0))

    counts = [number(r, 2 * MAXT) for r in range(GROUP)]
    lengths = [number(r, 2 * MAXT + 1) for r in range(GROUP)]
    slots = [[number(r, MAXT + at) for at in range(MAXT)] for r in range(GROUP)]
    for tile in range(TILES):
        slot = me * TILES + tile
        asker = jnp.int32(0)
        place = jnp.int32(0)
        length = lengths[0]
        for request in range(GROUP):
            for at in range(MAXT):
                hit = (slots[request][at] == slot) & (at < counts[request])
                asker = jnp.where(hit, request, asker)
                place = jnp.where(hit, at, place)
                length = jnp.where(hit, lengths[request], length)
        words = q_ref[asker, :, width:].astype(F32)
        column = lax.broadcasted_iota(jnp.int32, (PROMPT, HD), 1)
        seen = jnp.sum(jnp.where(column == place, words, 0.0), axis=1, keepdims=True)
        row = lax.broadcasted_iota(jnp.int32, (PROMPT, HD), 0)
        usable = (jnp.broadcast_to(seen, (PROMPT, HD)) > 0.5) & (row < length)
        for partner in range(GROUP):
            mine = lax.bitwise_xor(own, partner) == asker
            owned_ref[partner, tile] = jnp.where(usable & mine, 1.0, 0.0)
        for head in range(HEADS_HERE):
            for member in range(GSIZE):
                column = (head * GSIZE + member) * HD
                values = q_ref[asker, :, column : column + HD].astype(F32)
                squares = jnp.mean(values * values, axis=-1, keepdims=True)
                normed = values * lax.rsqrt(squares + 1e-05) * gain_ref[...]
                qn_ref[head, tile, member * PROMPT : (member + 1) * PROMPT, :] = normed.astype(BF16)


def prepare_queries(me, packed, query_gain):
    vmem = pl.BlockSpec(memory_space=pltpu.VMEM)
    return pl.pallas_call(
        query_kernel,
        in_specs=[pl.BlockSpec(memory_space=pltpu.SMEM), vmem, vmem],
        out_specs=[vmem, vmem],
        out_shape=[
            jax.ShapeDtypeStruct((HEADS_HERE, TILES, QROWS, HD), BF16),
            jax.ShapeDtypeStruct((GROUP, TILES, PROMPT, HD), F32),
        ],
        compiler_params=params(),
        cost_estimate=brief(),
        name="prepare_queries",
    )(me, packed, query_gain)


def attend(up, up_own, down, down_own, qn_ref, gain_ref, total_ref, scratch, skip, first):
    key_scr, value_scr = scratch
    for part, (got, own) in enumerate(((up, up_own), (down, down_own))):
        rows = got.shape[0] // 2
        both = (got[...].astype(F32) + own[...].astype(F32)).astype(BF16).astype(F32)
        key_scr[...] = both[:, :HD]
        value_scr[...] = both[:, HD:]
        for tile in range(TILES):
            keys = key_scr[pl.ds(tile, rows, stride=2), :]
            values = value_scr[pl.ds(tile, rows, stride=2), :]
            squares = jnp.mean(keys * keys, axis=-1, keepdims=True)
            keys = (keys * lax.rsqrt(squares + 1e-05) * gain_ref[...]).astype(BF16)
            ones = jnp.ones((rows, HD), F32)
            if part == 1 and skip:
                keep = lax.broadcasted_iota(jnp.int32, (rows, HD), 0) >= skip
                values = jnp.where(keep, values, 0.0)
                ones = jnp.where(keep, 1.0, 0.0)
            wide = jnp.concatenate([values, ones], axis=1).astype(BF16)
            scores = lax.dot_general(
                qn_ref[0, tile], keys, (((1,), (1,)), ((), ())), preferred_element_type=F32
            )
            weights = jnp.exp(scores * (1.0 / math.sqrt(HD))).astype(BF16)
            term = jnp.dot(weights, wide, preferred_element_type=F32)
            if first and part == 0:
                total_ref[tile] = term
            else:
                total_ref[tile] += term


def front_attention(parts, qn, key_gain):
    rows = parts[0].shape[0]

    def body(up, up_own, down, down_own, qn_ref, gain_ref, total_ref, *scratch):
        attend(
            up, up_own, down, down_own, qn_ref, gain_ref, total_ref.at[0], scratch, 0, True
        )

    return pl.pallas_call(
        body,
        grid=(HEADS_HERE,),
        in_specs=[pl.BlockSpec((rows, 2 * HD), lambda i: (0, i))] * 4
        + [
            pl.BlockSpec((1, TILES, QROWS, HD), lambda i: (i, 0, 0, 0)),
            pl.BlockSpec((1, HD), lambda i: (0, 0)),
        ],
        out_specs=pl.BlockSpec((1, TILES, QROWS, 2 * HD), lambda i: (i, 0, 0, 0)),
        out_shape=jax.ShapeDtypeStruct((HEADS_HERE, TILES, QROWS, 2 * HD), F32),
        scratch_shapes=[pltpu.VMEM((rows, HD), F32)] * 2,
        compiler_params=params(),
        cost_estimate=brief(),
        name="front_attention",
    )(*parts, qn, key_gain)


def diagonal(shape):
    row = lax.broadcasted_iota(jnp.int32, shape, 0)
    column = lax.broadcasted_iota(jnp.int32, shape, 1)
    return jnp.where(row == column, 1.0, 0.0).astype(F32)


def closing_attention(head, parts, qn, key_gain, before, owned, skip):
    rows = parts[0].shape[0]

    def body(
        up, up_own, down, down_own, qn_ref, gain_ref, before_ref, owned_ref, kept, *rest
    ):
        sent, (total_ref, key_scr, value_scr) = rest[: GROUP - 1], rest[GROUP - 1 :]
        total_ref[...] = before_ref[0]
        scratch = (key_scr, value_scr)
        attend(up, up_own, down, down_own, qn_ref, gain_ref, total_ref, scratch, skip, False)
        eye = diagonal((HD, HD))
        for partner in range(GROUP):
            rows_of = []
            for member in range(GSIZE):
                block = slice(member * PROMPT, (member + 1) * PROMPT)
                for part in range(2):
                    lanes = slice(part * HD, (part + 1) * HD)
                    held = jnp.zeros((PROMPT, HD), F32)
                    for tile in range(TILES):
                        belongs = owned_ref[partner, tile] > 0.5
                        held += jnp.where(belongs, total_ref[tile, block, lanes], 0.0)
                    if partner == 0:
                        kept[block, lanes] = held
                    elif part == 0:
                        sent[partner - 1][block, :] = held.astype(BF16)
                    else:
                        rows_of.append(held)
            if partner == 0:
                continue
            lines = []
            for at in range(QROWS // HD):
                square = jnp.concatenate([rows_of[2 * at], rows_of[2 * at + 1]], axis=0)
                lines.append(jnp.sum(square * eye, axis=0, keepdims=True))
            lines = jnp.concatenate(lines, axis=0)
            coarse = lines.astype(BF16).astype(F32)
            tail = jnp.concatenate([coarse, lines - coarse, jnp.zeros((8, HD), F32)], axis=0)
            sent[partner - 1][QROWS:, :] = tail.astype(BF16)

    whole = lambda *shape: pl.BlockSpec(shape, lambda i: (0,) * len(shape))
    own = pl.BlockSpec((rows, 2 * HD), lambda i: (0, head))
    return pl.pallas_call(
        body,
        grid=(1,),
        in_specs=[whole(rows, 2 * HD), own, whole(rows, 2 * HD), own]
        + [
            pl.BlockSpec((1, TILES, QROWS, HD), lambda i: (head, 0, 0, 0)),
            whole(1, HD),
            pl.BlockSpec((1, TILES, QROWS, 2 * HD), lambda i: (head, 0, 0, 0)),
            whole(GROUP, TILES, PROMPT, HD),
        ],
        out_specs=[whole(QROWS, 2 * HD)] + [whole(SENT_ROWS, HD)] * (GROUP - 1),
        out_shape=[jax.ShapeDtypeStruct((QROWS, 2 * HD), F32)]
        + [jax.ShapeDtypeStruct((SENT_ROWS, HD), BF16)] * (GROUP - 1),
        scratch_shapes=[pltpu.VMEM((TILES, QROWS, 2 * HD), F32)]
        + [pltpu.VMEM((rows, HD), F32)] * 2,
        compiler_params=params(),
        cost_estimate=brief(),
        name="closing_attention",
    )(*parts, qn, key_gain, before, owned)


def finish_kernel(info_ref, mask_ref, *refs):
    out_ref = refs[-1]
    lane = lax.broadcasted_iota(jnp.int32, (PROMPT, MAXT), 1)
    seen = jnp.where((lane < info_ref[0, 0]) & (mask_ref[0] == 1), 1, 0)
    seen = jnp.sum(seen, axis=1, keepdims=True)
    row = lax.broadcasted_iota(jnp.int32, (PROMPT, HD), 0)
    live = (jnp.broadcast_to(seen, (PROMPT, HD)) > 0) & (row < info_ref[0, 1])
    eye = diagonal((HD, HD))
    for head in range(HEADS_HERE):
        kept, *got = refs[head * GROUP : (head + 1) * GROUP]
        for at in range(QROWS // HD):
            line = jnp.zeros((1, HD), F32)
            for one in got:
                line += one[QROWS + at : QROWS + at + 1, :].astype(F32)
                line += one[QROWS + 4 + at : QROWS + 5 + at, :].astype(F32)
            square = jnp.broadcast_to(line, (HD, HD)) * eye
            spread = jnp.broadcast_to(jnp.sum(square, axis=1, keepdims=True), (HD, HD))
            block = slice(at * HD, (at + 1) * HD)
            numerator = kept[block, :HD]
            for one in got:
                numerator += one[block, :].astype(F32)
            denominator = kept[block, HD:] + spread
            for half in range(HD // PROMPT):
                inner = slice(half * PROMPT, (half + 1) * PROMPT)
                divisor = jnp.where(live, denominator[inner], 1.0)
                result = jnp.where(live, numerator[inner] / divisor, 0.0)
                column = (head * GSIZE + at * 2 + half) * HD
                out_ref[0, :, column : column + HD] = result.astype(BF16)


def finish(info, mask, parts):
    vmem = pl.BlockSpec(memory_space=pltpu.VMEM)
    return pl.pallas_call(
        finish_kernel,
        in_specs=[pl.BlockSpec(memory_space=pltpu.SMEM)] + [vmem] * (1 + len(parts)),
        out_specs=vmem,
        out_shape=jax.ShapeDtypeStruct((1, PROMPT, HEADS_HERE * GSIZE * HD), BF16),
        compiler_params=params(),
        cost_estimate=brief(),
        name="finish",
    )(info, mask, *parts)


def add(left, right):
    return (left.astype(F32) + right.astype(F32)).astype(BF16)


def local(
    tile_features,
    projection,
    queries,
    query_gain,
    key_gain,
    tile_count,
    tile_slot,
    cross_mask,
    prompt_length,
):
    own_index = lax.axis_index("dp")
    up_perm = [(i, (i + 1) % NHEAD) for i in range(NHEAD)]
    down_perm = [(i, (i - 1) % NHEAD) for i in range(NHEAD)]
    groups = [list(range(g, g + GROUP)) for g in range(0, lax.axis_size("dp"), GROUP)]
    info = jnp.concatenate([tile_count, prompt_length, tile_slot[0], jnp.zeros((2,), jnp.int32)])
    rows_first = jnp.transpose(tile_features, (1, 0, 2))
    perms = {"uf": up_perm, "ub": up_perm, "df": down_perm, "db": down_perm}
    names = (("uf", "df"), ("ub", "db"))
    running, held, arrived = {}, {}, {}
    later = NHEAD - 1

    def keep_later(start, outs):
        outs = iter(outs)
        for side in range(2):
            for at in range(start, min(2 * start + 1, later)):
                for pair in names:
                    held[pair[side], at] = next(outs)

    def hop(pair):
        for name in pair:
            running[name] = lax.ppermute(running[name], "head", perms[name])

    def last_hop(pair, heads, after=()):
        joined = join_heads(
            heads,
            [running[name] for name in pair],
            [held[name, 1] for name in pair],
            after,
            pair == back,
        )
        for name, one in zip(pair, joined):
            one = lax.ppermute(one, "head", perms[name])
            arrived[name, heads[0]] = one
        return joined

    front, back = names
    *outs, weights = open_ring(projection, rows_first)
    apart = {(name, head): outs[2 * n + head] for n, name in enumerate(front) for head in range(2)}
    parts = ((UP_BACK, BACK, ((0, BACK),)), (DOWN_BACK, BACK, ((0, BACK),)))
    running.update(zip(back, partials(rows_first, weights, parts, 1, 1)))
    whole = (
        (UP_FRONT, HALF, ((0, FRONT), (FRONT, BACK))),
        (DOWN_BACK, HALF, ((BACK, FRONT), (0, BACK))),
    )
    packed = pack_queries(info[None], cross_mask, queries, running["db"])
    packed = lax.all_gather(packed, "dp", axis=0, tiled=True, axis_index_groups=groups)
    for head in range(HEADS_HERE):
        for name in front:
            apart[name, head] = lax.ppermute(apart[name, head], "head", perms[name])
    low, high = [[apart[name, head] for name in front] for head in range(HEADS_HERE)]
    after = (running["db"], *low)
    keep_later(0, partials(rows_first, weights, whole, 2, 1, after))
    hop(back)
    running.update(zip(front, join_apart(low, high, [held[name, 0] for name in front])))
    for name in back:
        running[name] = add(running[name], held[name, 0])
    after = tuple(running[name] for name in front + back)
    keep_later(1, partials(rows_first, weights, whole, 3, 2, after))
    for pair in names:
        hop(pair)
    me = jnp.full((1,), own_index, jnp.int32)
    qn, owned = prepare_queries(me, packed, query_gain[None])
    key_line = key_gain[None]
    last = NHEAD - 2

    def parts_of(pair, head):
        up, down = pair
        return arrived[up, head], held[up, last], arrived[down, head], held[down, last]

    def send_back(sent):
        back = []
        for partner in range(1, GROUP):
            pairs = [(i, i ^ partner) for i in range(lax.axis_size("dp"))]
            back.append(lax.ppermute(sent[partner - 1], "dp", pairs))
        return back

    joined = last_hop(front, (0, 2), (qn,))
    joined = last_hop(back, (0, 1), tuple(joined))
    last_hop(back, (1, 2), tuple(joined))
    before = front_attention(parts_of(front, 0), qn, key_line)
    final = []
    for head in range(HEADS_HERE):
        kept, *sent = closing_attention(
            head, parts_of(back, head), qn, key_line, before, owned, OVERLAP
        )
        final += [kept] + send_back(sent)
    return finish(info[None], cross_mask, final)


def solution(mesh):
    in_specs = (
        P("dp", None, "head"),
        P("head", None, None),
        P("dp", None, "head"),
        P(),
        P(),
        P("dp"),
        P("dp", None),
        P("dp", None, None),
        P("dp"),
    )
    out_specs = P("dp", None, "head")
    return jax.shard_map(local, mesh=mesh, in_specs=in_specs, out_specs=out_specs, check_vma=False)
```

```python
import math

import jax
import jax.numpy as jnp
from jax import lax
from jax.experimental import pallas as pl
from jax.experimental.pallas import tpu as pltpu
from jax.sharding import PartitionSpec as P

KVH = 8
HD = 128
MAXT = 4
GROUP = 4
NHEAD = 4
GSIZE = 8
PROMPT = 64
QROWS = GSIZE * PROMPT
TROWS = 1601
WIDTH = 1920
TILES = 2
HEADS_HERE = 2
HALF = 808
FRONT = 448
BACK = HALF - FRONT
UP_FRONT, UP_BACK = 0, FRONT
DOWN_BACK, DOWN_FRONT = TROWS - HALF, TROWS - FRONT
OVERLAP = 2 * HALF - TROWS
SENT_ROWS = QROWS + 16
F32 = jnp.float32
BF16 = jnp.bfloat16
VMEM_LIMIT = 56 * 2**20
VMEM_ALL = 64 * 2**20
PAIR = 4 * HD
CUTS = (0, 768, 1536, WIDTH)


def params(limit=VMEM_LIMIT):
    return pltpu.CompilerParams(vmem_limit_bytes=limit)


def brief():
    return pl.CostEstimate(flops=2**10, bytes_accessed=2**10, transcendentals=0)


def lasting():
    return pl.CostEstimate(flops=10**11, bytes_accessed=2**24, transcendentals=0)


def shard_at(side, step):
    here = lax.axis_index("head")
    return lax.rem(here + (NHEAD - step if side == 0 else step), NHEAD)


def open_ring_kernel(w_hbm, x_hbm, *refs):
    outs, wt_hbm = refs[:4], refs[4]
    raw, turned, held, totals, raw_sem, out_sem, x_sem = refs[5:]

    def raw_copy(at):
        depth = pl.ds(CUTS[at], CUTS[at + 1] - CUTS[at])
        return pltpu.make_async_copy(w_hbm.at[depth], raw.at[depth], raw_sem.at[at])

    def turned_copy(at):
        depth = pl.ds(CUTS[at], CUTS[at + 1] - CUTS[at])
        return pltpu.make_async_copy(turned.at[:, depth], wt_hbm.at[:, depth], out_sem.at[at])

    def row_copy(side):
        start = (UP_FRONT, DOWN_FRONT)[side]
        return pltpu.make_async_copy(x_hbm.at[pl.ds(start, FRONT)], held.at[side], x_sem.at[side])

    chunks = len(CUTS) - 1
    row_copy(0).start()
    raw_copy(0).start()
    row_copy(1).start()
    for at in range(1, chunks):
        raw_copy(at).start()
    shards = [shard_at(side, 1) for side in range(2)]
    for at in range(chunks):
        low, high = CUTS[at], CUTS[at + 1]
        raw_copy(at).wait()
        lines = jnp.transpose(raw[low:high], (1, 0, 2))
        for head in range(KVH):
            lanes = slice(head % 2 * 2 * HD, (head % 2 + 1) * 2 * HD)
            turned[head // 2, low:high, lanes] = lines[head]
        turned_copy(at).start()
        for side in range(2):
            if at == 0:
                row_copy(side).wait()
            flat = held[side, :, :, low:high].reshape(2 * FRONT, high - low)
            term = jnp.dot(flat, turned[shards[side], low:high], preferred_element_type=F32)
            if at > 0:
                term = totals[side] + term
            if at < chunks - 1:
                totals[side] = term
            else:
                outs[2 * side][...] = term[:, : 2 * HD].astype(BF16)
                outs[2 * side + 1][...] = term[:, 2 * HD :].astype(BF16)
    for at in range(chunks):
        turned_copy(at).wait()


def open_ring(projection, rows_first):
    hbm = pl.BlockSpec(memory_space=pl.ANY)
    vmem = pl.BlockSpec(memory_space=pltpu.VMEM)
    chunks = len(CUTS) - 1
    return pl.pallas_call(
        open_ring_kernel,
        in_specs=[hbm, hbm],
        out_specs=[vmem] * 4 + [hbm],
        out_shape=[jax.ShapeDtypeStruct((2 * FRONT, 2 * HD), BF16)] * 4
        + [jax.ShapeDtypeStruct((NHEAD, WIDTH, PAIR), BF16)],
        scratch_shapes=[
            pltpu.VMEM((WIDTH, KVH, 2 * HD), BF16),
            pltpu.VMEM((NHEAD, WIDTH, PAIR), BF16),
            pltpu.VMEM((2, FRONT, TILES, WIDTH), BF16),
            pltpu.VMEM((2, 2 * FRONT, PAIR), F32),
            pltpu.SemaphoreType.DMA((chunks,)),
            pltpu.SemaphoreType.DMA((chunks,)),
            pltpu.SemaphoreType.DMA((2,)),
        ],
        compiler_params=params(),
        cost_estimate=brief(),
        name="open_ring",
    )(projection, rows_first)


def partials_kernel(parts, start, steps, waits, x_hbm, w_hbm, *refs):
    refs = refs[waits:]
    sides = len(parts)
    many = sum(len(part[2]) for part in parts) * steps
    outs, (held, flat, weights, ready, x_sem, w_sem, out_sem) = refs[:many], refs[many:]

    def row_copy(side):
        first, count = parts[side][:2]
        return pltpu.make_async_copy(
            x_hbm.at[pl.ds(first, count)], held.at[side, pl.ds(0, count)], x_sem.at[side]
        )

    def weight_copy(side, step):
        n = side * steps + step
        shard = shard_at(side, start + step)
        return pltpu.make_async_copy(w_hbm.at[shard], weights.at[n], w_sem.at[n])

    for side in range(sides):
        row_copy(side).start()
        for step in range(steps):
            weight_copy(side, step).start()
    copies = []
    for side, (_, count, cuts) in enumerate(parts):
        row_copy(side).wait()
        flat[: 2 * count] = held[side, :count].reshape(2 * count, WIDTH)
        for step in range(steps):
            weight_copy(side, step).wait()
            slot = side * steps + step
            ready[slot, : 2 * count] = jnp.dot(
                flat[: 2 * count], weights[slot], preferred_element_type=F32
            ).astype(BF16)
            for first, size in cuts:
                n = len(copies)
                rows = pl.ds(2 * first, 2 * size)
                copies.append(pltpu.make_async_copy(ready.at[slot, rows], outs[n], out_sem.at[n]))
                copies[-1].start()
    for copy in copies:
        copy.wait()


def partials(rows_first, weights, parts, start, steps, after=()):
    sides = len(parts)
    most = max(part[1] for part in parts)
    sizes = [size for part in parts for _ in range(steps) for first, size in part[2]]
    hbm = pl.BlockSpec(memory_space=pl.ANY)
    return pl.pallas_call(
        lambda *refs: partials_kernel(parts, start, steps, len(after), *refs),
        in_specs=[hbm] * (2 + len(after)),
        out_specs=[hbm] * len(sizes),
        out_shape=[jax.ShapeDtypeStruct((2 * size, PAIR), BF16) for size in sizes],
        scratch_shapes=[
            pltpu.VMEM((sides, most, TILES, WIDTH), BF16),
            pltpu.VMEM((2 * most, WIDTH), BF16),
            pltpu.VMEM((sides * steps, WIDTH, PAIR), BF16),
            pltpu.VMEM((sides * steps, 2 * most, PAIR), BF16),
            pltpu.SemaphoreType.DMA((sides,)),
            pltpu.SemaphoreType.DMA((sides * steps,)),
            pltpu.SemaphoreType.DMA((len(sizes),)),
        ],
        compiler_params=params(),
        cost_estimate=lasting(),
        name="partials",
    )(rows_first, weights, *after)


def join_apart(low, high, own):
    many = len(own)

    def body(*refs):
        for n in range(many):
            for head in range(HEADS_HERE):
                lanes = slice(head * 2 * HD, (head + 1) * 2 * HD)
                total = refs[head * many + n][...].astype(F32)
                total += refs[2 * many + n][:, lanes].astype(F32)
                refs[3 * many + n][:, lanes] = total.astype(BF16)

    vmem = pl.BlockSpec(memory_space=pltpu.VMEM)
    return pl.pallas_call(
        body,
        in_specs=[vmem] * (3 * many),
        out_specs=[vmem] * many,
        out_shape=[jax.ShapeDtypeStruct(one.shape, BF16) for one in own],
        compiler_params=params(),
        cost_estimate=brief(),
        name="join_apart",
    )(*low, *high, *own)


def join_heads(heads, got, own, after, slow):
    many = len(got)
    width = (heads[1] - heads[0]) * 2 * HD

    def body(*refs):
        for n in range(many):
            total = refs[n][...].astype(F32) + refs[many + n][...].astype(F32)
            refs[2 * many + len(after) + n][...] = total.astype(BF16)

    def spec(one, at):
        return pl.BlockSpec((one.shape[0], width), lambda i: (0, at))

    return pl.pallas_call(
        body,
        grid=(1,),
        in_specs=[spec(one, heads[0]) for one in got + own]
        + [pl.BlockSpec(memory_space=pl.ANY)] * len(after),
        out_specs=[spec(one, 0) for one in got],
        out_shape=[jax.ShapeDtypeStruct((one.shape[0], width), BF16) for one in got],
        compiler_params=params(),
        cost_estimate=lasting() if slow else brief(),
        name="join_heads",
    )(*got, *own, *after)


def pack_kernel(info_ref, mask_ref, q_ref, after_ref, out_ref):
    out_ref[0, :, : q_ref.shape[2]] = q_ref[0]
    lane = lax.broadcasted_iota(jnp.int32, (PROMPT, HD), 1)
    words = jnp.zeros((PROMPT, HD), jnp.int32)
    for at in range(MAXT):
        words = jnp.where(lane == at, mask_ref[0, :, at : at + 1], words)
        words = jnp.where(lane == MAXT + at, info_ref[0, 2 + at], words)
    words = jnp.where(lane == 2 * MAXT, info_ref[0, 0], words)
    words = jnp.where(lane == 2 * MAXT + 1, info_ref[0, 1], words)
    out_ref[0, :, q_ref.shape[2] :] = words.astype(F32).astype(BF16)


def pack_queries(info, mask, queries, after):
    vmem = pl.BlockSpec(memory_space=pltpu.VMEM)
    width = queries.shape[2] + HD
    return pl.pallas_call(
        pack_kernel,
        in_specs=[
            pl.BlockSpec(memory_space=pltpu.SMEM),
            vmem,
            vmem,
            pl.BlockSpec(memory_space=pl.ANY),
        ],
        out_specs=vmem,
        out_shape=jax.ShapeDtypeStruct((1, PROMPT, width), BF16),
        compiler_params=params(),
        cost_estimate=brief(),
        name="pack_queries",
    )(info, mask, queries, after)


def query_kernel(me_ref, q_ref, gain_ref, qn_ref, owned_ref):
    me = me_ref[0]
    own = lax.rem(me, GROUP)
    width = q_ref.shape[2] - HD
    lane = lax.broadcasted_iota(jnp.int32, (1, HD), 1)

    def number(request, at):
        line = q_ref[request, 0:16, width:].astype(F32).astype(jnp.int32)[0:1]
        return jnp.sum(jnp.where(lane == at, line, 0))

    counts = [number(r, 2 * MAXT) for r in range(GROUP)]
    lengths = [number(r, 2 * MAXT + 1) for r in range(GROUP)]
    slots = [[number(r, MAXT + at) for at in range(MAXT)] for r in range(GROUP)]
    for tile in range(TILES):
        slot = me * TILES + tile
        asker = jnp.int32(0)
        place = jnp.int32(0)
        length = lengths[0]
        for request in range(GROUP):
            for at in range(MAXT):
                hit = (slots[request][at] == slot) & (at < counts[request])
                asker = jnp.where(hit, request, asker)
                place = jnp.where(hit, at, place)
                length = jnp.where(hit, lengths[request], length)
        words = q_ref[asker, :, width:].astype(F32)
        column = lax.broadcasted_iota(jnp.int32, (PROMPT, HD), 1)
        seen = jnp.sum(jnp.where(column == place, words, 0.0), axis=1, keepdims=True)
        row = lax.broadcasted_iota(jnp.int32, (PROMPT, HD), 0)
        usable = (jnp.broadcast_to(seen, (PROMPT, HD)) > 0.5) & (row < length)
        for partner in range(GROUP):
            mine = lax.bitwise_xor(own, partner) == asker
            owned_ref[partner, tile] = jnp.where(usable & mine, 1.0, 0.0)
        for head in range(HEADS_HERE):
            for member in range(GSIZE):
                column = (head * GSIZE + member) * HD
                values = q_ref[asker, :, column : column + HD].astype(F32)
                squares = jnp.mean(values * values, axis=-1, keepdims=True)
                normed = values * lax.rsqrt(squares + 1e-05) * gain_ref[...]
                qn_ref[head, tile, member * PROMPT : (member + 1) * PROMPT, :] = normed.astype(BF16)


def prepare_queries(me, packed, query_gain):
    vmem = pl.BlockSpec(memory_space=pltpu.VMEM)
    return pl.pallas_call(
        query_kernel,
        in_specs=[pl.BlockSpec(memory_space=pltpu.SMEM), vmem, vmem],
        out_specs=[vmem, vmem],
        out_shape=[
            jax.ShapeDtypeStruct((HEADS_HERE, TILES, QROWS, HD), BF16),
            jax.ShapeDtypeStruct((GROUP, TILES, PROMPT, HD), F32),
        ],
        compiler_params=params(),
        cost_estimate=brief(),
        name="prepare_queries",
    )(me, packed, query_gain)


def attend(up, up_own, down, down_own, qn_ref, gain_ref, total_ref, scratch, skip, first):
    key_scr, value_scr = scratch
    for part, (got, own) in enumerate(((up, up_own), (down, down_own))):
        rows = got.shape[0] // 2
        both = (got[...].astype(F32) + own[...].astype(F32)).astype(BF16).astype(F32)
        key_scr[...] = both[:, :HD]
        value_scr[...] = both[:, HD:]
        for tile in range(TILES):
            keys = key_scr[pl.ds(tile, rows, stride=2), :]
            values = value_scr[pl.ds(tile, rows, stride=2), :]
            squares = jnp.mean(keys * keys, axis=-1, keepdims=True)
            keys = (keys * lax.rsqrt(squares + 1e-05) * gain_ref[...]).astype(BF16)
            ones = jnp.ones((rows, HD), F32)
            if part == 1 and skip:
                keep = lax.broadcasted_iota(jnp.int32, (rows, HD), 0) >= skip
                values = jnp.where(keep, values, 0.0)
                ones = jnp.where(keep, 1.0, 0.0)
            wide = jnp.concatenate([values, ones], axis=1).astype(BF16)
            scores = lax.dot_general(
                qn_ref[0, tile], keys, (((1,), (1,)), ((), ())), preferred_element_type=F32
            )
            weights = jnp.exp(scores * (1.0 / math.sqrt(HD))).astype(BF16)
            term = jnp.dot(weights, wide, preferred_element_type=F32)
            if first and part == 0:
                total_ref[tile] = term
            else:
                total_ref[tile] += term


def front_attention(parts, qn, key_gain):
    rows = parts[0].shape[0]

    def body(up, up_own, down, down_own, qn_ref, gain_ref, total_ref, *scratch):
        attend(
            up, up_own, down, down_own, qn_ref, gain_ref, total_ref.at[0], scratch, 0, True
        )

    return pl.pallas_call(
        body,
        grid=(HEADS_HERE,),
        in_specs=[pl.BlockSpec((rows, 2 * HD), lambda i: (0, i))] * 4
        + [
            pl.BlockSpec((1, TILES, QROWS, HD), lambda i: (i, 0, 0, 0)),
            pl.BlockSpec((1, HD), lambda i: (0, 0)),
        ],
        out_specs=pl.BlockSpec((1, TILES, QROWS, 2 * HD), lambda i: (i, 0, 0, 0)),
        out_shape=jax.ShapeDtypeStruct((HEADS_HERE, TILES, QROWS, 2 * HD), F32),
        scratch_shapes=[pltpu.VMEM((rows, HD), F32)] * 2,
        compiler_params=params(VMEM_ALL),
        cost_estimate=brief(),
        name="front_attention",
    )(*parts, qn, key_gain)


def diagonal(shape):
    row = lax.broadcasted_iota(jnp.int32, shape, 0)
    column = lax.broadcasted_iota(jnp.int32, shape, 1)
    return jnp.where(row == column, 1.0, 0.0).astype(F32)


def closing_attention(head, parts, qn, key_gain, before, owned, skip):
    rows = parts[0].shape[0]

    def body(
        up, up_own, down, down_own, qn_ref, gain_ref, before_ref, owned_ref, kept, *rest
    ):
        sent, (total_ref, key_scr, value_scr) = rest[: GROUP - 1], rest[GROUP - 1 :]
        total_ref[...] = before_ref[0]
        scratch = (key_scr, value_scr)
        attend(up, up_own, down, down_own, qn_ref, gain_ref, total_ref, scratch, skip, False)
        eye = diagonal((HD, HD))
        for partner in range(GROUP):
            rows_of = []
            for member in range(GSIZE):
                block = slice(member * PROMPT, (member + 1) * PROMPT)
                for part in range(2):
                    lanes = slice(part * HD, (part + 1) * HD)
                    held = jnp.zeros((PROMPT, HD), F32)
                    for tile in range(TILES):
                        belongs = owned_ref[partner, tile] > 0.5
                        held += jnp.where(belongs, total_ref[tile, block, lanes], 0.0)
                    if partner == 0:
                        kept[block, lanes] = held
                    elif part == 0:
                        sent[partner - 1][block, :] = held.astype(BF16)
                    else:
                        rows_of.append(held)
            if partner == 0:
                continue
            lines = []
            for at in range(QROWS // HD):
                square = jnp.concatenate([rows_of[2 * at], rows_of[2 * at + 1]], axis=0)
                lines.append(jnp.sum(square * eye, axis=0, keepdims=True))
            lines = jnp.concatenate(lines, axis=0)
            coarse = lines.astype(BF16).astype(F32)
            tail = jnp.concatenate([coarse, lines - coarse, jnp.zeros((8, HD), F32)], axis=0)
            sent[partner - 1][QROWS:, :] = tail.astype(BF16)

    whole = lambda *shape: pl.BlockSpec(shape, lambda i: (0,) * len(shape))
    own = pl.BlockSpec((rows, 2 * HD), lambda i: (0, head))
    return pl.pallas_call(
        body,
        grid=(1,),
        in_specs=[whole(rows, 2 * HD), own, whole(rows, 2 * HD), own]
        + [
            pl.BlockSpec((1, TILES, QROWS, HD), lambda i: (head, 0, 0, 0)),
            whole(1, HD),
            pl.BlockSpec((1, TILES, QROWS, 2 * HD), lambda i: (head, 0, 0, 0)),
            whole(GROUP, TILES, PROMPT, HD),
        ],
        out_specs=[whole(QROWS, 2 * HD)] + [whole(SENT_ROWS, HD)] * (GROUP - 1),
        out_shape=[jax.ShapeDtypeStruct((QROWS, 2 * HD), F32)]
        + [jax.ShapeDtypeStruct((SENT_ROWS, HD), BF16)] * (GROUP - 1),
        scratch_shapes=[pltpu.VMEM((TILES, QROWS, 2 * HD), F32)]
        + [pltpu.VMEM((rows, HD), F32)] * 2,
        compiler_params=params(VMEM_ALL),
        cost_estimate=brief(),
        name="closing_attention",
    )(*parts, qn, key_gain, before, owned)


def finish_kernel(info_ref, mask_ref, *refs):
    out_ref = refs[-1]
    lane = lax.broadcasted_iota(jnp.int32, (PROMPT, MAXT), 1)
    seen = jnp.where((lane < info_ref[0, 0]) & (mask_ref[0] == 1), 1, 0)
    seen = jnp.sum(seen, axis=1, keepdims=True)
    row = lax.broadcasted_iota(jnp.int32, (PROMPT, HD), 0)
    live = (jnp.broadcast_to(seen, (PROMPT, HD)) > 0) & (row < info_ref[0, 1])
    eye = diagonal((HD, HD))
    for head in range(HEADS_HERE):
        kept, *got = refs[head * GROUP : (head + 1) * GROUP]
        for at in range(QROWS // HD):
            line = jnp.zeros((1, HD), F32)
            for one in got:
                line += one[QROWS + at : QROWS + at + 1, :].astype(F32)
                line += one[QROWS + 4 + at : QROWS + 5 + at, :].astype(F32)
            square = jnp.broadcast_to(line, (HD, HD)) * eye
            spread = jnp.broadcast_to(jnp.sum(square, axis=1, keepdims=True), (HD, HD))
            block = slice(at * HD, (at + 1) * HD)
            numerator = kept[block, :HD]
            for one in got:
                numerator += one[block, :].astype(F32)
            denominator = kept[block, HD:] + spread
            for half in range(HD // PROMPT):
                inner = slice(half * PROMPT, (half + 1) * PROMPT)
                divisor = jnp.where(live, denominator[inner], 1.0)
                result = jnp.where(live, numerator[inner] / divisor, 0.0)
                column = (head * GSIZE + at * 2 + half) * HD
                out_ref[0, :, column : column + HD] = result.astype(BF16)


def finish(info, mask, parts):
    vmem = pl.BlockSpec(memory_space=pltpu.VMEM)
    return pl.pallas_call(
        finish_kernel,
        in_specs=[pl.BlockSpec(memory_space=pltpu.SMEM)] + [vmem] * (1 + len(parts)),
        out_specs=vmem,
        out_shape=jax.ShapeDtypeStruct((1, PROMPT, HEADS_HERE * GSIZE * HD), BF16),
        compiler_params=params(VMEM_ALL),
        cost_estimate=brief(),
        name="finish",
    )(info, mask, *parts)


def add(left, right):
    return (left.astype(F32) + right.astype(F32)).astype(BF16)


def local(
    tile_features,
    projection,
    queries,
    query_gain,
    key_gain,
    tile_count,
    tile_slot,
    cross_mask,
    prompt_length,
):
    own_index = lax.axis_index("dp")
    up_perm = [(i, (i + 1) % NHEAD) for i in range(NHEAD)]
    down_perm = [(i, (i - 1) % NHEAD) for i in range(NHEAD)]
    groups = [list(range(g, g + GROUP)) for g in range(0, lax.axis_size("dp"), GROUP)]
    info = jnp.concatenate([tile_count, prompt_length, tile_slot[0], jnp.zeros((2,), jnp.int32)])
    rows_first = jnp.transpose(tile_features, (1, 0, 2))
    perms = {"uf": up_perm, "ub": up_perm, "df": down_perm, "db": down_perm}
    names = (("uf", "df"), ("ub", "db"))
    running, held, arrived = {}, {}, {}
    later = NHEAD - 1

    def keep_later(start, outs):
        outs = iter(outs)
        for side in range(2):
            for at in range(start, min(2 * start + 1, later)):
                for pair in names:
                    held[pair[side], at] = next(outs)

    def hop(pair):
        for name in pair:
            running[name] = lax.ppermute(running[name], "head", perms[name])

    def last_hop(pair, heads, after=()):
        joined = join_heads(
            heads,
            [running[name] for name in pair],
            [held[name, 1] for name in pair],
            after,
            pair == back,
        )
        for name, one in zip(pair, joined):
            one = lax.ppermute(one, "head", perms[name])
            arrived[name, heads[0]] = one
        return joined

    front, back = names
    *outs, weights = open_ring(projection, rows_first)
    apart = {(name, head): outs[2 * n + head] for n, name in enumerate(front) for head in range(2)}
    parts = ((UP_BACK, BACK, ((0, BACK),)), (DOWN_BACK, BACK, ((0, BACK),)))
    running.update(zip(back, partials(rows_first, weights, parts, 1, 1)))
    whole = (
        (UP_FRONT, HALF, ((0, FRONT), (FRONT, BACK))),
        (DOWN_BACK, HALF, ((BACK, FRONT), (0, BACK))),
    )
    packed = pack_queries(info[None], cross_mask, queries, running["db"])
    packed = lax.all_gather(packed, "dp", axis=0, tiled=True, axis_index_groups=groups)
    for head in range(HEADS_HERE):
        for name in front:
            apart[name, head] = lax.ppermute(apart[name, head], "head", perms[name])
    low, high = [[apart[name, head] for name in front] for head in range(HEADS_HERE)]
    after = (running["db"], *low)
    keep_later(0, partials(rows_first, weights, whole, 2, 1, after))
    hop(back)
    running.update(zip(front, join_apart(low, high, [held[name, 0] for name in front])))
    for name in back:
        running[name] = add(running[name], held[name, 0])
    after = tuple(running[name] for name in front + back)
    keep_later(1, partials(rows_first, weights, whole, 3, 2, after))
    for pair in names:
        hop(pair)
    me = jnp.full((1,), own_index, jnp.int32)
    qn, owned = prepare_queries(me, packed, query_gain[None])
    key_line = key_gain[None]
    last = NHEAD - 2

    def parts_of(pair, head):
        up, down = pair
        return arrived[up, head], held[up, last], arrived[down, head], held[down, last]

    def send_back(sent):
        back = []
        for partner in (2, 3, 1):
            pairs = [(i, i ^ partner) for i in range(lax.axis_size("dp"))]
            back.append(lax.ppermute(sent[partner - 1], "dp", pairs))
        return back

    joined = last_hop(front, (0, 2), (qn,))
    joined = last_hop(back, (0, 1), tuple(joined))
    last_hop(back, (1, 2), tuple(joined))
    before = front_attention(parts_of(front, 0), qn, key_line)
    final = []
    for head in range(HEADS_HERE):
        kept, *sent = closing_attention(
            head, parts_of(back, head), qn, key_line, before, owned, OVERLAP
        )
        final += [kept] + send_back(sent)
    return finish(info[None], cross_mask, final)


def solution(mesh):
    in_specs = (
        P("dp", None, "head"),
        P("head", None, None),
        P("dp", None, "head"),
        P(),
        P(),
        P("dp"),
        P("dp", None),
        P("dp", None, None),
        P("dp"),
    )
    out_specs = P("dp", None, "head")
    return jax.shard_map(local, mesh=mesh, in_specs=in_specs, out_specs=out_specs, check_vma=False)
```

```python
import math

import jax
import jax.numpy as jnp
from jax import lax
from jax.experimental import pallas as pl
from jax.experimental.pallas import tpu as pltpu
from jax.sharding import PartitionSpec as P

KVH = 8
HD = 128
MAXT = 4
GROUP = 4
NHEAD = 4
GSIZE = 8
PROMPT = 64
QROWS = GSIZE * PROMPT
TROWS = 1601
WIDTH = 1920
TILES = 2
HEADS_HERE = 2
HALF = 808
FRONT = 448
BACK = HALF - FRONT
UP_FRONT, UP_BACK = 0, FRONT
DOWN_BACK, DOWN_FRONT = TROWS - HALF, TROWS - FRONT
OVERLAP = 2 * HALF - TROWS
SENT_ROWS = QROWS + 16
F32 = jnp.float32
BF16 = jnp.bfloat16
VMEM_LIMIT = 56 * 2**20
VMEM_ALL = 64 * 2**20
PAIR = 4 * HD
CUTS = (0, 768, 1536, WIDTH)


def params(limit=VMEM_LIMIT):
    return pltpu.CompilerParams(vmem_limit_bytes=limit)


def brief():
    return pl.CostEstimate(flops=2**10, bytes_accessed=2**10, transcendentals=0)


def lasting():
    return pl.CostEstimate(flops=10**11, bytes_accessed=2**24, transcendentals=0)


def shard_at(side, step):
    here = lax.axis_index("head")
    return lax.rem(here + (NHEAD - step if side == 0 else step), NHEAD)


def open_ring_kernel(w_hbm, x_hbm, *refs):
    outs, wt_hbm = refs[:4], refs[4]
    raw, turned, held, totals, raw_sem, out_sem, x_sem = refs[5:]

    def raw_copy(at):
        depth = pl.ds(CUTS[at], CUTS[at + 1] - CUTS[at])
        return pltpu.make_async_copy(w_hbm.at[depth], raw.at[depth], raw_sem.at[at])

    def turned_copy(at):
        depth = pl.ds(CUTS[at], CUTS[at + 1] - CUTS[at])
        return pltpu.make_async_copy(turned.at[:, depth], wt_hbm.at[:, depth], out_sem.at[at])

    def row_copy(side):
        start = (UP_FRONT, DOWN_FRONT)[side]
        return pltpu.make_async_copy(x_hbm.at[pl.ds(start, FRONT)], held.at[side], x_sem.at[side])

    chunks = len(CUTS) - 1
    row_copy(0).start()
    raw_copy(0).start()
    row_copy(1).start()
    for at in range(1, chunks):
        raw_copy(at).start()
    shards = [shard_at(side, 1) for side in range(2)]
    for at in range(chunks):
        low, high = CUTS[at], CUTS[at + 1]
        raw_copy(at).wait()
        lines = jnp.transpose(raw[low:high], (1, 0, 2))
        for head in range(KVH):
            lanes = slice(head % 2 * 2 * HD, (head % 2 + 1) * 2 * HD)
            turned[head // 2, low:high, lanes] = lines[head]
        turned_copy(at).start()
        for side in range(2):
            if at == 0:
                row_copy(side).wait()
            flat = held[side, :, :, low:high].reshape(2 * FRONT, high - low)
            term = jnp.dot(flat, turned[shards[side], low:high], preferred_element_type=F32)
            if at > 0:
                term = totals[side] + term
            if at < chunks - 1:
                totals[side] = term
            else:
                outs[2 * side][...] = term[:, : 2 * HD].astype(BF16)
                outs[2 * side + 1][...] = term[:, 2 * HD :].astype(BF16)
    for at in range(chunks):
        turned_copy(at).wait()


def open_ring(projection, rows_first):
    hbm = pl.BlockSpec(memory_space=pl.ANY)
    vmem = pl.BlockSpec(memory_space=pltpu.VMEM)
    chunks = len(CUTS) - 1
    return pl.pallas_call(
        open_ring_kernel,
        in_specs=[hbm, hbm],
        out_specs=[vmem] * 4 + [hbm],
        out_shape=[jax.ShapeDtypeStruct((2 * FRONT, 2 * HD), BF16)] * 4
        + [jax.ShapeDtypeStruct((NHEAD, WIDTH, PAIR), BF16)],
        scratch_shapes=[
            pltpu.VMEM((WIDTH, KVH, 2 * HD), BF16),
            pltpu.VMEM((NHEAD, WIDTH, PAIR), BF16),
            pltpu.VMEM((2, FRONT, TILES, WIDTH), BF16),
            pltpu.VMEM((2, 2 * FRONT, PAIR), F32),
            pltpu.SemaphoreType.DMA((chunks,)),
            pltpu.SemaphoreType.DMA((chunks,)),
            pltpu.SemaphoreType.DMA((2,)),
        ],
        compiler_params=params(),
        cost_estimate=brief(),
        name="open_ring",
    )(projection, rows_first)


def partials_kernel(parts, start, steps, waits, x_hbm, w_hbm, *refs):
    refs = refs[waits:]
    sides = len(parts)
    many = sum(len(part[2]) for part in parts) * steps
    outs, (held, flat, weights, ready, x_sem, w_sem, out_sem) = refs[:many], refs[many:]

    def row_copy(side):
        first, count = parts[side][:2]
        return pltpu.make_async_copy(
            x_hbm.at[pl.ds(first, count)], held.at[side, pl.ds(0, count)], x_sem.at[side]
        )

    def weight_copy(side, step):
        n = side * steps + step
        shard = shard_at(side, start + step)
        return pltpu.make_async_copy(w_hbm.at[shard], weights.at[n], w_sem.at[n])

    for side in range(sides):
        row_copy(side).start()
        for step in range(steps):
            weight_copy(side, step).start()
    copies = []
    for side, (_, count, cuts) in enumerate(parts):
        row_copy(side).wait()
        flat[: 2 * count] = held[side, :count].reshape(2 * count, WIDTH)
        for step in range(steps):
            weight_copy(side, step).wait()
            slot = side * steps + step
            ready[slot, : 2 * count] = jnp.dot(
                flat[: 2 * count], weights[slot], preferred_element_type=F32
            ).astype(BF16)
            for first, size in cuts:
                n = len(copies)
                rows = pl.ds(2 * first, 2 * size)
                copies.append(pltpu.make_async_copy(ready.at[slot, rows], outs[n], out_sem.at[n]))
                copies[-1].start()
    for copy in copies:
        copy.wait()


def partials(rows_first, weights, parts, start, steps, after=()):
    sides = len(parts)
    most = max(part[1] for part in parts)
    sizes = [size for part in parts for _ in range(steps) for first, size in part[2]]
    hbm = pl.BlockSpec(memory_space=pl.ANY)
    return pl.pallas_call(
        lambda *refs: partials_kernel(parts, start, steps, len(after), *refs),
        in_specs=[hbm] * (2 + len(after)),
        out_specs=[hbm] * len(sizes),
        out_shape=[jax.ShapeDtypeStruct((2 * size, PAIR), BF16) for size in sizes],
        scratch_shapes=[
            pltpu.VMEM((sides, most, TILES, WIDTH), BF16),
            pltpu.VMEM((2 * most, WIDTH), BF16),
            pltpu.VMEM((sides * steps, WIDTH, PAIR), BF16),
            pltpu.VMEM((sides * steps, 2 * most, PAIR), BF16),
            pltpu.SemaphoreType.DMA((sides,)),
            pltpu.SemaphoreType.DMA((sides * steps,)),
            pltpu.SemaphoreType.DMA((len(sizes),)),
        ],
        compiler_params=params(),
        cost_estimate=lasting(),
        name="partials",
    )(rows_first, weights, *after)


def join_apart(low, high, own):
    many = len(own)

    def body(*refs):
        for n in range(many):
            for head in range(HEADS_HERE):
                lanes = slice(head * 2 * HD, (head + 1) * 2 * HD)
                total = refs[head * many + n][...].astype(F32)
                total += refs[2 * many + n][:, lanes].astype(F32)
                refs[3 * many + n][:, lanes] = total.astype(BF16)

    vmem = pl.BlockSpec(memory_space=pltpu.VMEM)
    return pl.pallas_call(
        body,
        in_specs=[vmem] * (3 * many),
        out_specs=[vmem] * many,
        out_shape=[jax.ShapeDtypeStruct(one.shape, BF16) for one in own],
        compiler_params=params(),
        cost_estimate=brief(),
        name="join_apart",
    )(*low, *high, *own)


def join_heads(heads, got, own, after, slow):
    many = len(got)
    width = (heads[1] - heads[0]) * 2 * HD

    def body(*refs):
        for n in range(many):
            total = refs[n][...].astype(F32) + refs[many + n][...].astype(F32)
            refs[2 * many + len(after) + n][...] = total.astype(BF16)

    def spec(one, at):
        return pl.BlockSpec((one.shape[0], width), lambda i: (0, at))

    return pl.pallas_call(
        body,
        grid=(1,),
        in_specs=[spec(one, heads[0]) for one in got + own]
        + [pl.BlockSpec(memory_space=pl.ANY)] * len(after),
        out_specs=[spec(one, 0) for one in got],
        out_shape=[jax.ShapeDtypeStruct((one.shape[0], width), BF16) for one in got],
        compiler_params=params(),
        cost_estimate=lasting() if slow else brief(),
        name="join_heads",
    )(*got, *own, *after)


def pack_kernel(info_ref, mask_ref, q_ref, after_ref, out_ref):
    out_ref[0, :, : q_ref.shape[2]] = q_ref[0]
    lane = lax.broadcasted_iota(jnp.int32, (PROMPT, HD), 1)
    words = jnp.zeros((PROMPT, HD), jnp.int32)
    for at in range(MAXT):
        words = jnp.where(lane == at, mask_ref[0, :, at : at + 1], words)
        words = jnp.where(lane == MAXT + at, info_ref[0, 2 + at], words)
    words = jnp.where(lane == 2 * MAXT, info_ref[0, 0], words)
    words = jnp.where(lane == 2 * MAXT + 1, info_ref[0, 1], words)
    out_ref[0, :, q_ref.shape[2] :] = words.astype(F32).astype(BF16)


def pack_queries(info, mask, queries, after):
    vmem = pl.BlockSpec(memory_space=pltpu.VMEM)
    width = queries.shape[2] + HD
    return pl.pallas_call(
        pack_kernel,
        in_specs=[
            pl.BlockSpec(memory_space=pltpu.SMEM),
            vmem,
            vmem,
            pl.BlockSpec(memory_space=pl.ANY),
        ],
        out_specs=vmem,
        out_shape=jax.ShapeDtypeStruct((1, PROMPT, width), BF16),
        compiler_params=params(),
        cost_estimate=brief(),
        name="pack_queries",
    )(info, mask, queries, after)


def query_kernel(me_ref, q_ref, gain_ref, qn_ref, owned_ref):
    me = me_ref[0]
    own = lax.rem(me, GROUP)
    width = q_ref.shape[2] - HD
    lane = lax.broadcasted_iota(jnp.int32, (1, HD), 1)

    def number(request, at):
        line = q_ref[request, 0:16, width:].astype(F32).astype(jnp.int32)[0:1]
        return jnp.sum(jnp.where(lane == at, line, 0))

    counts = [number(r, 2 * MAXT) for r in range(GROUP)]
    lengths = [number(r, 2 * MAXT + 1) for r in range(GROUP)]
    slots = [[number(r, MAXT + at) for at in range(MAXT)] for r in range(GROUP)]
    for tile in range(TILES):
        slot = me * TILES + tile
        asker = jnp.int32(0)
        place = jnp.int32(0)
        length = lengths[0]
        for request in range(GROUP):
            for at in range(MAXT):
                hit = (slots[request][at] == slot) & (at < counts[request])
                asker = jnp.where(hit, request, asker)
                place = jnp.where(hit, at, place)
                length = jnp.where(hit, lengths[request], length)
        words = q_ref[asker, :, width:].astype(F32)
        column = lax.broadcasted_iota(jnp.int32, (PROMPT, HD), 1)
        seen = jnp.sum(jnp.where(column == place, words, 0.0), axis=1, keepdims=True)
        row = lax.broadcasted_iota(jnp.int32, (PROMPT, HD), 0)
        usable = (jnp.broadcast_to(seen, (PROMPT, HD)) > 0.5) & (row < length)
        for partner in range(GROUP):
            mine = lax.bitwise_xor(own, partner) == asker
            owned_ref[partner, tile] = jnp.where(usable & mine, 1.0, 0.0)
        for head in range(HEADS_HERE):
            for member in range(GSIZE):
                column = (head * GSIZE + member) * HD
                values = q_ref[asker, :, column : column + HD].astype(F32)
                squares = jnp.mean(values * values, axis=-1, keepdims=True)
                normed = values * lax.rsqrt(squares + 1e-05) * gain_ref[...]
                qn_ref[head, tile, member * PROMPT : (member + 1) * PROMPT, :] = normed.astype(BF16)


def prepare_queries(me, packed, query_gain):
    vmem = pl.BlockSpec(memory_space=pltpu.VMEM)
    return pl.pallas_call(
        query_kernel,
        in_specs=[pl.BlockSpec(memory_space=pltpu.SMEM), vmem, vmem],
        out_specs=[vmem, vmem],
        out_shape=[
            jax.ShapeDtypeStruct((HEADS_HERE, TILES, QROWS, HD), BF16),
            jax.ShapeDtypeStruct((GROUP, TILES, PROMPT, HD), F32),
        ],
        compiler_params=params(),
        cost_estimate=brief(),
        name="prepare_queries",
    )(me, packed, query_gain)


def attend(up, up_own, down, down_own, qn_ref, gain_ref, total_ref, scratch, skip, first):
    key_scr, value_scr = scratch
    for part, (got, own) in enumerate(((up, up_own), (down, down_own))):
        rows = got.shape[0] // 2
        both = (got[...].astype(F32) + own[...].astype(F32)).astype(BF16).astype(F32)
        key_scr[...] = both[:, :HD]
        value_scr[...] = both[:, HD:]
        for tile in range(TILES):
            keys = key_scr[pl.ds(tile, rows, stride=2), :]
            values = value_scr[pl.ds(tile, rows, stride=2), :]
            squares = jnp.mean(keys * keys, axis=-1, keepdims=True)
            keys = (keys * lax.rsqrt(squares + 1e-05) * gain_ref[...]).astype(BF16)
            ones = jnp.ones((rows, HD), F32)
            if part == 1 and skip:
                keep = lax.broadcasted_iota(jnp.int32, (rows, HD), 0) >= skip
                values = jnp.where(keep, values, 0.0)
                ones = jnp.where(keep, 1.0, 0.0)
            wide = jnp.concatenate([values, ones], axis=1).astype(BF16)
            scores = lax.dot_general(
                qn_ref[0, tile], keys, (((1,), (1,)), ((), ())), preferred_element_type=F32
            )
            weights = jnp.exp(scores * (1.0 / math.sqrt(HD))).astype(BF16)
            term = jnp.dot(weights, wide, preferred_element_type=F32)
            if first and part == 0:
                total_ref[tile] = term
            else:
                total_ref[tile] += term


def front_attention(parts, qn, key_gain):
    rows = parts[0].shape[0]

    def body(up, up_own, down, down_own, qn_ref, gain_ref, total_ref, *scratch):
        attend(
            up, up_own, down, down_own, qn_ref, gain_ref, total_ref.at[0], scratch, 0, True
        )

    return pl.pallas_call(
        body,
        grid=(HEADS_HERE,),
        in_specs=[pl.BlockSpec((rows, 2 * HD), lambda i: (0, i))] * 4
        + [
            pl.BlockSpec((1, TILES, QROWS, HD), lambda i: (i, 0, 0, 0)),
            pl.BlockSpec((1, HD), lambda i: (0, 0)),
        ],
        out_specs=pl.BlockSpec((1, TILES, QROWS, 2 * HD), lambda i: (i, 0, 0, 0)),
        out_shape=jax.ShapeDtypeStruct((HEADS_HERE, TILES, QROWS, 2 * HD), F32),
        scratch_shapes=[pltpu.VMEM((rows, HD), F32)] * 2,
        compiler_params=params(VMEM_ALL),
        cost_estimate=brief(),
        name="front_attention",
    )(*parts, qn, key_gain)


def diagonal(shape):
    row = lax.broadcasted_iota(jnp.int32, shape, 0)
    column = lax.broadcasted_iota(jnp.int32, shape, 1)
    return jnp.where(row == column, 1.0, 0.0).astype(F32)


def closing_attention(head, parts, qn, key_gain, before, owned, skip):
    rows = parts[0].shape[0]

    def body(
        up, up_own, down, down_own, qn_ref, gain_ref, before_ref, owned_ref, kept, *rest
    ):
        sent, (total_ref, key_scr, value_scr) = rest[: GROUP - 1], rest[GROUP - 1 :]
        total_ref[...] = before_ref[0]
        scratch = (key_scr, value_scr)
        attend(up, up_own, down, down_own, qn_ref, gain_ref, total_ref, scratch, skip, False)
        eye = diagonal((HD, HD))
        for partner in range(GROUP):
            rows_of = []
            for member in range(GSIZE):
                block = slice(member * PROMPT, (member + 1) * PROMPT)
                for part in range(2):
                    lanes = slice(part * HD, (part + 1) * HD)
                    held = jnp.zeros((PROMPT, HD), F32)
                    for tile in range(TILES):
                        belongs = owned_ref[partner, tile] > 0.5
                        held += jnp.where(belongs, total_ref[tile, block, lanes], 0.0)
                    if partner == 0:
                        kept[block, lanes] = held
                    elif part == 0:
                        sent[partner - 1][block, :] = held.astype(BF16)
                    else:
                        rows_of.append(held)
            if partner == 0:
                continue
            lines = []
            for at in range(QROWS // HD):
                square = jnp.concatenate([rows_of[2 * at], rows_of[2 * at + 1]], axis=0)
                lines.append(jnp.sum(square * eye, axis=0, keepdims=True))
            lines = jnp.concatenate(lines, axis=0)
            coarse = lines.astype(BF16).astype(F32)
            tail = jnp.concatenate([coarse, lines - coarse, jnp.zeros((8, HD), F32)], axis=0)
            sent[partner - 1][QROWS:, :] = tail.astype(BF16)

    whole = lambda *shape: pl.BlockSpec(shape, lambda i: (0,) * len(shape))
    own = pl.BlockSpec((rows, 2 * HD), lambda i: (0, head))
    return pl.pallas_call(
        body,
        grid=(1,),
        in_specs=[whole(rows, 2 * HD), own, whole(rows, 2 * HD), own]
        + [
            pl.BlockSpec((1, TILES, QROWS, HD), lambda i: (head, 0, 0, 0)),
            whole(1, HD),
            pl.BlockSpec((1, TILES, QROWS, 2 * HD), lambda i: (head, 0, 0, 0)),
            whole(GROUP, TILES, PROMPT, HD),
        ],
        out_specs=[whole(QROWS, 2 * HD)] + [whole(SENT_ROWS, HD)] * (GROUP - 1),
        out_shape=[jax.ShapeDtypeStruct((QROWS, 2 * HD), F32)]
        + [jax.ShapeDtypeStruct((SENT_ROWS, HD), BF16)] * (GROUP - 1),
        scratch_shapes=[pltpu.VMEM((TILES, QROWS, 2 * HD), F32)]
        + [pltpu.VMEM((rows, HD), F32)] * 2,
        compiler_params=params(VMEM_ALL),
        cost_estimate=brief(),
        name="closing_attention",
    )(*parts, qn, key_gain, before, owned)


def finish_kernel(info_ref, mask_ref, *refs):
    out_ref = refs[-1]
    lane = lax.broadcasted_iota(jnp.int32, (PROMPT, MAXT), 1)
    seen = jnp.where((lane < info_ref[0, 0]) & (mask_ref[0] == 1), 1, 0)
    seen = jnp.sum(seen, axis=1, keepdims=True)
    row = lax.broadcasted_iota(jnp.int32, (PROMPT, HD), 0)
    live = (jnp.broadcast_to(seen, (PROMPT, HD)) > 0) & (row < info_ref[0, 1])
    eye = diagonal((HD, HD))
    for head in range(HEADS_HERE):
        kept, *got = refs[head * GROUP : (head + 1) * GROUP]
        for at in range(QROWS // HD):
            line = jnp.zeros((1, HD), F32)
            for one in got:
                line += one[QROWS + at : QROWS + at + 1, :].astype(F32)
                line += one[QROWS + 4 + at : QROWS + 5 + at, :].astype(F32)
            square = jnp.broadcast_to(line, (HD, HD)) * eye
            spread = jnp.broadcast_to(jnp.sum(square, axis=1, keepdims=True), (HD, HD))
            block = slice(at * HD, (at + 1) * HD)
            numerator = kept[block, :HD]
            for one in got:
                numerator += one[block, :].astype(F32)
            denominator = kept[block, HD:] + spread
            for half in range(HD // PROMPT):
                inner = slice(half * PROMPT, (half + 1) * PROMPT)
                divisor = jnp.where(live, denominator[inner], 1.0)
                result = jnp.where(live, numerator[inner] / divisor, 0.0)
                column = (head * GSIZE + at * 2 + half) * HD
                out_ref[0, :, column : column + HD] = result.astype(BF16)


def finish(info, mask, parts):
    vmem = pl.BlockSpec(memory_space=pltpu.VMEM)
    return pl.pallas_call(
        finish_kernel,
        in_specs=[pl.BlockSpec(memory_space=pltpu.SMEM)] + [vmem] * (1 + len(parts)),
        out_specs=vmem,
        out_shape=jax.ShapeDtypeStruct((1, PROMPT, HEADS_HERE * GSIZE * HD), BF16),
        compiler_params=params(VMEM_ALL),
        cost_estimate=brief(),
        name="finish",
    )(info, mask, *parts)


def add(left, right):
    return (left.astype(F32) + right.astype(F32)).astype(BF16)


def local(
    tile_features,
    projection,
    queries,
    query_gain,
    key_gain,
    tile_count,
    tile_slot,
    cross_mask,
    prompt_length,
):
    own_index = lax.axis_index("dp")
    up_perm = [(i, (i + 1) % NHEAD) for i in range(NHEAD)]
    down_perm = [(i, (i - 1) % NHEAD) for i in range(NHEAD)]
    groups = [list(range(g, g + GROUP)) for g in range(0, lax.axis_size("dp"), GROUP)]
    info = jnp.concatenate([tile_count, prompt_length, tile_slot[0], jnp.zeros((2,), jnp.int32)])
    rows_first = jnp.transpose(tile_features, (1, 0, 2))
    perms = {"uf": up_perm, "ub": up_perm, "df": down_perm, "db": down_perm}
    names = (("uf", "df"), ("ub", "db"))
    running, held, arrived = {}, {}, {}
    later = NHEAD - 1

    def keep_later(start, outs):
        outs = iter(outs)
        for side in range(2):
            for at in range(start, min(2 * start + 1, later)):
                for pair in names:
                    held[pair[side], at] = next(outs)

    def hop(pair):
        for name in pair:
            running[name] = lax.ppermute(running[name], "head", perms[name])

    def last_hop(pair, heads, after=()):
        joined = join_heads(
            heads,
            [running[name] for name in pair],
            [held[name, 1] for name in pair],
            after,
            pair == back,
        )
        for name, one in zip(pair, joined):
            one = lax.ppermute(one, "head", perms[name])
            arrived[name, heads[0]] = one
        return joined

    front, back = names
    *outs, weights = open_ring(projection, rows_first)
    apart = {(name, head): outs[2 * n + head] for n, name in enumerate(front) for head in range(2)}
    parts = ((UP_BACK, BACK, ((0, BACK),)), (DOWN_BACK, BACK, ((0, BACK),)))
    running.update(zip(back, partials(rows_first, weights, parts, 1, 1)))
    whole = (
        (UP_FRONT, HALF, ((0, FRONT), (FRONT, BACK))),
        (DOWN_BACK, HALF, ((BACK, FRONT), (0, BACK))),
    )
    for head in range(HEADS_HERE):
        for name in front:
            apart[name, head] = lax.ppermute(apart[name, head], "head", perms[name])
    low, high = [[apart[name, head] for name in front] for head in range(HEADS_HERE)]
    after = (running["db"], *low)
    keep_later(0, partials(rows_first, weights, whole, 2, 1, after))
    hop(back)
    running.update(zip(front, join_apart(low, high, [held[name, 0] for name in front])))
    for name in back:
        running[name] = add(running[name], held[name, 0])
    after = tuple(running[name] for name in front + back)
    keep_later(1, partials(rows_first, weights, whole, 3, 2, after))
    packed = pack_queries(info[None], cross_mask, queries, held["df", 1])
    packed = lax.all_gather(packed, "dp", axis=0, tiled=True, axis_index_groups=groups)
    for pair in names:
        hop(pair)
    me = jnp.full((1,), own_index, jnp.int32)
    qn, owned = prepare_queries(me, packed, query_gain[None])
    key_line = key_gain[None]
    last = NHEAD - 2

    def parts_of(pair, head):
        up, down = pair
        return arrived[up, head], held[up, last], arrived[down, head], held[down, last]

    def send_back(sent):
        back = []
        for partner in (2, 3, 1):
            pairs = [(i, i ^ partner) for i in range(lax.axis_size("dp"))]
            back.append(lax.ppermute(sent[partner - 1], "dp", pairs))
        return back

    joined = last_hop(front, (0, 2))
    joined = last_hop(back, (0, 1), tuple(joined))
    last_hop(back, (1, 2), (*joined, qn))
    before = front_attention(parts_of(front, 0), qn, key_line)
    final = []
    for head in range(HEADS_HERE):
        kept, *sent = closing_attention(
            head, parts_of(back, head), qn, key_line, before, owned, OVERLAP
        )
        final += [kept] + send_back(sent)
    return finish(info[None], cross_mask, final)


def solution(mesh):
    in_specs = (
        P("dp", None, "head"),
        P("head", None, None),
        P("dp", None, "head"),
        P(),
        P(),
        P("dp"),
        P("dp", None),
        P("dp", None, None),
        P("dp"),
    )
    out_specs = P("dp", None, "head")
    return jax.shard_map(local, mesh=mesh, in_specs=in_specs, out_specs=out_specs, check_vma=False)
```

```python
import math

import jax
import jax.numpy as jnp
from jax import lax
from jax.experimental import pallas as pl
from jax.experimental.pallas import tpu as pltpu
from jax.sharding import PartitionSpec as P

KVH = 8
HD = 128
MAXT = 4
GROUP = 4
NHEAD = 4
GSIZE = 8
PROMPT = 64
QROWS = GSIZE * PROMPT
TROWS = 1601
WIDTH = 1920
TILES = 2
HEADS_HERE = 2
HALF = 808
FRONT = 448
BACK = HALF - FRONT
UP_FRONT, UP_BACK = 0, FRONT
DOWN_BACK, DOWN_FRONT = TROWS - HALF, TROWS - FRONT
OVERLAP = 2 * HALF - TROWS
SENT_ROWS = QROWS + 16
F32 = jnp.float32
BF16 = jnp.bfloat16
VMEM_LIMIT = 56 * 2**20
VMEM_ALL = 64 * 2**20
PAIR = 4 * HD
CUTS = (0, 768, 1536, WIDTH)


def params(limit=VMEM_LIMIT):
    return pltpu.CompilerParams(vmem_limit_bytes=limit)


def brief():
    return pl.CostEstimate(flops=2**10, bytes_accessed=2**10, transcendentals=0)


def lasting():
    return pl.CostEstimate(flops=10**11, bytes_accessed=2**24, transcendentals=0)


def shard_at(side, step):
    here = lax.axis_index("head")
    return lax.rem(here + (NHEAD - step if side == 0 else step), NHEAD)


def open_ring_kernel(w_hbm, x_hbm, *refs):
    outs, wt_hbm = refs[:4], refs[4]
    raw, turned, held, totals, raw_sem, out_sem, x_sem = refs[5:]

    def raw_copy(at):
        depth = pl.ds(CUTS[at], CUTS[at + 1] - CUTS[at])
        return pltpu.make_async_copy(w_hbm.at[depth], raw.at[depth], raw_sem.at[at])

    def turned_copy(at):
        depth = pl.ds(CUTS[at], CUTS[at + 1] - CUTS[at])
        return pltpu.make_async_copy(turned.at[:, depth], wt_hbm.at[:, depth], out_sem.at[at])

    def row_copy(side):
        start = (UP_FRONT, DOWN_FRONT)[side]
        return pltpu.make_async_copy(x_hbm.at[pl.ds(start, FRONT)], held.at[side], x_sem.at[side])

    chunks = len(CUTS) - 1
    row_copy(0).start()
    raw_copy(0).start()
    row_copy(1).start()
    for at in range(1, chunks):
        raw_copy(at).start()
    shards = [shard_at(side, 1) for side in range(2)]
    for at in range(chunks):
        low, high = CUTS[at], CUTS[at + 1]
        raw_copy(at).wait()
        lines = jnp.transpose(raw[low:high], (1, 0, 2))
        for head in range(KVH):
            lanes = slice(head % 2 * 2 * HD, (head % 2 + 1) * 2 * HD)
            turned[head // 2, low:high, lanes] = lines[head]
        turned_copy(at).start()
        for side in range(2):
            if at == 0:
                row_copy(side).wait()
            flat = held[side, :, :, low:high].reshape(2 * FRONT, high - low)
            term = jnp.dot(flat, turned[shards[side], low:high], preferred_element_type=F32)
            if at > 0:
                term = totals[side] + term
            if at < chunks - 1:
                totals[side] = term
            else:
                outs[2 * side][...] = term[:, : 2 * HD].astype(BF16)
                outs[2 * side + 1][...] = term[:, 2 * HD :].astype(BF16)
    for at in range(chunks):
        turned_copy(at).wait()


def open_ring(projection, rows_first):
    hbm = pl.BlockSpec(memory_space=pl.ANY)
    vmem = pl.BlockSpec(memory_space=pltpu.VMEM)
    chunks = len(CUTS) - 1
    return pl.pallas_call(
        open_ring_kernel,
        in_specs=[hbm, hbm],
        out_specs=[vmem] * 4 + [hbm],
        out_shape=[jax.ShapeDtypeStruct((2 * FRONT, 2 * HD), BF16)] * 4
        + [jax.ShapeDtypeStruct((NHEAD, WIDTH, PAIR), BF16)],
        scratch_shapes=[
            pltpu.VMEM((WIDTH, KVH, 2 * HD), BF16),
            pltpu.VMEM((NHEAD, WIDTH, PAIR), BF16),
            pltpu.VMEM((2, FRONT, TILES, WIDTH), BF16),
            pltpu.VMEM((2, 2 * FRONT, PAIR), F32),
            pltpu.SemaphoreType.DMA((chunks,)),
            pltpu.SemaphoreType.DMA((chunks,)),
            pltpu.SemaphoreType.DMA((2,)),
        ],
        compiler_params=params(),
        cost_estimate=brief(),
        name="open_ring",
    )(projection, rows_first)


def partials_kernel(parts, start, steps, waits, x_hbm, w_hbm, *refs):
    refs = refs[waits:]
    sides = len(parts)
    many = sum(len(part[2]) for part in parts) * steps
    outs, (held, flat, weights, ready, x_sem, w_sem, out_sem) = refs[:many], refs[many:]

    def row_copy(side):
        first, count = parts[side][:2]
        return pltpu.make_async_copy(
            x_hbm.at[pl.ds(first, count)], held.at[side, pl.ds(0, count)], x_sem.at[side]
        )

    def weight_copy(side, step):
        n = side * steps + step
        shard = shard_at(side, start + step)
        return pltpu.make_async_copy(w_hbm.at[shard], weights.at[n], w_sem.at[n])

    for side in range(sides):
        row_copy(side).start()
        for step in range(steps):
            weight_copy(side, step).start()
    copies = []
    for side, (_, count, cuts) in enumerate(parts):
        row_copy(side).wait()
        flat[: 2 * count] = held[side, :count].reshape(2 * count, WIDTH)
        for step in range(steps):
            weight_copy(side, step).wait()
            slot = side * steps + step
            ready[slot, : 2 * count] = jnp.dot(
                flat[: 2 * count], weights[slot], preferred_element_type=F32
            ).astype(BF16)
            for first, size in cuts:
                n = len(copies)
                rows = pl.ds(2 * first, 2 * size)
                copies.append(pltpu.make_async_copy(ready.at[slot, rows], outs[n], out_sem.at[n]))
                copies[-1].start()
    for copy in copies:
        copy.wait()


def partials(rows_first, weights, parts, start, steps, after=()):
    sides = len(parts)
    most = max(part[1] for part in parts)
    sizes = [size for part in parts for _ in range(steps) for first, size in part[2]]
    hbm = pl.BlockSpec(memory_space=pl.ANY)
    return pl.pallas_call(
        lambda *refs: partials_kernel(parts, start, steps, len(after), *refs),
        in_specs=[hbm] * (2 + len(after)),
        out_specs=[hbm] * len(sizes),
        out_shape=[jax.ShapeDtypeStruct((2 * size, PAIR), BF16) for size in sizes],
        scratch_shapes=[
            pltpu.VMEM((sides, most, TILES, WIDTH), BF16),
            pltpu.VMEM((2 * most, WIDTH), BF16),
            pltpu.VMEM((sides * steps, WIDTH, PAIR), BF16),
            pltpu.VMEM((sides * steps, 2 * most, PAIR), BF16),
            pltpu.SemaphoreType.DMA((sides,)),
            pltpu.SemaphoreType.DMA((sides * steps,)),
            pltpu.SemaphoreType.DMA((len(sizes),)),
        ],
        compiler_params=params(),
        cost_estimate=lasting(),
        name="partials",
    )(rows_first, weights, *after)


def join_apart(low, high, own):
    many = len(own)

    def body(*refs):
        for n in range(many):
            for head in range(HEADS_HERE):
                lanes = slice(head * 2 * HD, (head + 1) * 2 * HD)
                total = refs[head * many + n][...].astype(F32)
                total += refs[2 * many + n][:, lanes].astype(F32)
                refs[3 * many + n][:, lanes] = total.astype(BF16)

    vmem = pl.BlockSpec(memory_space=pltpu.VMEM)
    return pl.pallas_call(
        body,
        in_specs=[vmem] * (3 * many),
        out_specs=[vmem] * many,
        out_shape=[jax.ShapeDtypeStruct(one.shape, BF16) for one in own],
        compiler_params=params(),
        cost_estimate=brief(),
        name="join_apart",
    )(*low, *high, *own)


def join_heads(heads, got, own, after, slow):
    many = len(got)
    width = (heads[1] - heads[0]) * 2 * HD

    def body(*refs):
        for n in range(many):
            total = refs[n][...].astype(F32) + refs[many + n][...].astype(F32)
            refs[2 * many + len(after) + n][...] = total.astype(BF16)

    def spec(one, at):
        return pl.BlockSpec((one.shape[0], width), lambda i: (0, at))

    return pl.pallas_call(
        body,
        grid=(1,),
        in_specs=[spec(one, heads[0]) for one in got + own]
        + [pl.BlockSpec(memory_space=pl.ANY)] * len(after),
        out_specs=[spec(one, 0) for one in got],
        out_shape=[jax.ShapeDtypeStruct((one.shape[0], width), BF16) for one in got],
        compiler_params=params(),
        cost_estimate=lasting() if slow else brief(),
        name="join_heads",
    )(*got, *own, *after)


def pack_kernel(info_ref, mask_ref, q_ref, after_ref, out_ref):
    out_ref[0, :, : q_ref.shape[2]] = q_ref[0]
    lane = lax.broadcasted_iota(jnp.int32, (PROMPT, HD), 1)
    words = jnp.zeros((PROMPT, HD), jnp.int32)
    for at in range(MAXT):
        words = jnp.where(lane == at, mask_ref[0, :, at : at + 1], words)
        words = jnp.where(lane == MAXT + at, info_ref[0, 2 + at], words)
    words = jnp.where(lane == 2 * MAXT, info_ref[0, 0], words)
    words = jnp.where(lane == 2 * MAXT + 1, info_ref[0, 1], words)
    out_ref[0, :, q_ref.shape[2] :] = words.astype(F32).astype(BF16)


def pack_queries(info, mask, queries, after):
    vmem = pl.BlockSpec(memory_space=pltpu.VMEM)
    width = queries.shape[2] + HD
    return pl.pallas_call(
        pack_kernel,
        in_specs=[
            pl.BlockSpec(memory_space=pltpu.SMEM),
            vmem,
            vmem,
            pl.BlockSpec(memory_space=pl.ANY),
        ],
        out_specs=vmem,
        out_shape=jax.ShapeDtypeStruct((1, PROMPT, width), BF16),
        compiler_params=params(),
        cost_estimate=brief(),
        name="pack_queries",
    )(info, mask, queries, after)


def query_kernel(me_ref, q_ref, gain_ref, qn_ref, owned_ref):
    me = me_ref[0]
    own = lax.rem(me, GROUP)
    width = q_ref.shape[2] - HD
    lane = lax.broadcasted_iota(jnp.int32, (1, HD), 1)

    def number(request, at):
        line = q_ref[request, 0:16, width:].astype(F32).astype(jnp.int32)[0:1]
        return jnp.sum(jnp.where(lane == at, line, 0))

    counts = [number(r, 2 * MAXT) for r in range(GROUP)]
    lengths = [number(r, 2 * MAXT + 1) for r in range(GROUP)]
    slots = [[number(r, MAXT + at) for at in range(MAXT)] for r in range(GROUP)]
    for tile in range(TILES):
        slot = me * TILES + tile
        asker = jnp.int32(0)
        place = jnp.int32(0)
        length = lengths[0]
        for request in range(GROUP):
            for at in range(MAXT):
                hit = (slots[request][at] == slot) & (at < counts[request])
                asker = jnp.where(hit, request, asker)
                place = jnp.where(hit, at, place)
                length = jnp.where(hit, lengths[request], length)
        words = q_ref[asker, :, width:].astype(F32)
        column = lax.broadcasted_iota(jnp.int32, (PROMPT, HD), 1)
        seen = jnp.sum(jnp.where(column == place, words, 0.0), axis=1, keepdims=True)
        row = lax.broadcasted_iota(jnp.int32, (PROMPT, HD), 0)
        usable = (jnp.broadcast_to(seen, (PROMPT, HD)) > 0.5) & (row < length)
        for partner in range(GROUP):
            mine = lax.bitwise_xor(own, partner) == asker
            owned_ref[partner, tile] = jnp.where(usable & mine, 1.0, 0.0)
        for head in range(HEADS_HERE):
            for member in range(GSIZE):
                column = (head * GSIZE + member) * HD
                values = q_ref[asker, :, column : column + HD].astype(F32)
                squares = jnp.mean(values * values, axis=-1, keepdims=True)
                normed = values * lax.rsqrt(squares + 1e-05) * gain_ref[...]
                qn_ref[head, tile, member * PROMPT : (member + 1) * PROMPT, :] = normed.astype(BF16)


def prepare_queries(me, packed, query_gain):
    vmem = pl.BlockSpec(memory_space=pltpu.VMEM)
    return pl.pallas_call(
        query_kernel,
        in_specs=[pl.BlockSpec(memory_space=pltpu.SMEM), vmem, vmem],
        out_specs=[vmem, vmem],
        out_shape=[
            jax.ShapeDtypeStruct((HEADS_HERE, TILES, QROWS, HD), BF16),
            jax.ShapeDtypeStruct((GROUP, TILES, PROMPT, HD), F32),
        ],
        compiler_params=params(),
        cost_estimate=brief(),
        name="prepare_queries",
    )(me, packed, query_gain)


def attend(up, up_own, down, down_own, qn_ref, gain_ref, total_ref, scratch, skip, first):
    key_scr, value_scr = scratch
    for part, (got, own) in enumerate(((up, up_own), (down, down_own))):
        rows = got.shape[0] // 2
        both = (got[...].astype(F32) + own[...].astype(F32)).astype(BF16).astype(F32)
        key_scr[...] = both[:, :HD]
        value_scr[...] = both[:, HD:]
        for tile in range(TILES):
            keys = key_scr[pl.ds(tile, rows, stride=2), :]
            values = value_scr[pl.ds(tile, rows, stride=2), :]
            squares = jnp.mean(keys * keys, axis=-1, keepdims=True)
            keys = (keys * lax.rsqrt(squares + 1e-05) * gain_ref[...]).astype(BF16)
            ones = jnp.ones((rows, HD), F32)
            if part == 1 and skip:
                keep = lax.broadcasted_iota(jnp.int32, (rows, HD), 0) >= skip
                values = jnp.where(keep, values, 0.0)
                ones = jnp.where(keep, 1.0, 0.0)
            wide = jnp.concatenate([values, ones], axis=1).astype(BF16)
            scores = lax.dot_general(
                qn_ref[0, tile], keys, (((1,), (1,)), ((), ())), preferred_element_type=F32
            )
            weights = jnp.exp(scores * (1.0 / math.sqrt(HD))).astype(BF16)
            term = jnp.dot(weights, wide, preferred_element_type=F32)
            if first and part == 0:
                total_ref[tile] = term
            else:
                total_ref[tile] += term


def front_attention(parts, qn, key_gain):
    rows = parts[0].shape[0]

    def body(up, up_own, down, down_own, qn_ref, gain_ref, total_ref, *scratch):
        attend(
            up, up_own, down, down_own, qn_ref, gain_ref, total_ref.at[0], scratch, 0, True
        )

    return pl.pallas_call(
        body,
        grid=(HEADS_HERE,),
        in_specs=[pl.BlockSpec((rows, 2 * HD), lambda i: (0, i))] * 4
        + [
            pl.BlockSpec((1, TILES, QROWS, HD), lambda i: (i, 0, 0, 0)),
            pl.BlockSpec((1, HD), lambda i: (0, 0)),
        ],
        out_specs=pl.BlockSpec((1, TILES, QROWS, 2 * HD), lambda i: (i, 0, 0, 0)),
        out_shape=jax.ShapeDtypeStruct((HEADS_HERE, TILES, QROWS, 2 * HD), F32),
        scratch_shapes=[pltpu.VMEM((rows, HD), F32)] * 2,
        compiler_params=params(VMEM_ALL),
        cost_estimate=brief(),
        name="front_attention",
    )(*parts, qn, key_gain)


def diagonal(shape):
    row = lax.broadcasted_iota(jnp.int32, shape, 0)
    column = lax.broadcasted_iota(jnp.int32, shape, 1)
    return jnp.where(row == column, 1.0, 0.0).astype(F32)


def closing_attention(head, parts, qn, key_gain, before, owned, skip):
    rows = parts[0].shape[0]

    def body(
        up, up_own, down, down_own, qn_ref, gain_ref, before_ref, owned_ref, kept, *rest
    ):
        sent, (total_ref, key_scr, value_scr) = rest[: GROUP - 1], rest[GROUP - 1 :]
        total_ref[...] = before_ref[0]
        scratch = (key_scr, value_scr)
        attend(up, up_own, down, down_own, qn_ref, gain_ref, total_ref, scratch, skip, False)
        eye = diagonal((HD, HD))
        for partner in range(GROUP):
            rows_of = []
            for member in range(GSIZE):
                block = slice(member * PROMPT, (member + 1) * PROMPT)
                for part in range(2):
                    lanes = slice(part * HD, (part + 1) * HD)
                    held = jnp.zeros((PROMPT, HD), F32)
                    for tile in range(TILES):
                        belongs = owned_ref[partner, tile] > 0.5
                        held += jnp.where(belongs, total_ref[tile, block, lanes], 0.0)
                    if partner == 0:
                        kept[block, lanes] = held
                    elif part == 0:
                        sent[partner - 1][block, :] = held.astype(BF16)
                    else:
                        rows_of.append(held)
            if partner == 0:
                continue
            lines = []
            for at in range(QROWS // HD):
                square = jnp.concatenate([rows_of[2 * at], rows_of[2 * at + 1]], axis=0)
                lines.append(jnp.sum(square * eye, axis=0, keepdims=True))
            lines = jnp.concatenate(lines, axis=0)
            coarse = lines.astype(BF16).astype(F32)
            tail = jnp.concatenate([coarse, lines - coarse, jnp.zeros((8, HD), F32)], axis=0)
            sent[partner - 1][QROWS:, :] = tail.astype(BF16)

    whole = lambda *shape: pl.BlockSpec(shape, lambda i: (0,) * len(shape))
    own = pl.BlockSpec((rows, 2 * HD), lambda i: (0, head))
    return pl.pallas_call(
        body,
        grid=(1,),
        in_specs=[whole(rows, 2 * HD), own, whole(rows, 2 * HD), own]
        + [
            pl.BlockSpec((1, TILES, QROWS, HD), lambda i: (head, 0, 0, 0)),
            whole(1, HD),
            pl.BlockSpec((1, TILES, QROWS, 2 * HD), lambda i: (head, 0, 0, 0)),
            whole(GROUP, TILES, PROMPT, HD),
        ],
        out_specs=[whole(QROWS, 2 * HD)] + [whole(SENT_ROWS, HD)] * (GROUP - 1),
        out_shape=[jax.ShapeDtypeStruct((QROWS, 2 * HD), F32)]
        + [jax.ShapeDtypeStruct((SENT_ROWS, HD), BF16)] * (GROUP - 1),
        scratch_shapes=[pltpu.VMEM((TILES, QROWS, 2 * HD), F32)]
        + [pltpu.VMEM((rows, HD), F32)] * 2,
        compiler_params=params(VMEM_ALL),
        cost_estimate=brief(),
        name="closing_attention",
    )(*parts, qn, key_gain, before, owned)


def finish_kernel(info_ref, mask_ref, *refs):
    out_ref = refs[-1]
    lane = lax.broadcasted_iota(jnp.int32, (PROMPT, MAXT), 1)
    seen = jnp.where((lane < info_ref[0, 0]) & (mask_ref[0] == 1), 1, 0)
    seen = jnp.sum(seen, axis=1, keepdims=True)
    row = lax.broadcasted_iota(jnp.int32, (PROMPT, HD), 0)
    live = (jnp.broadcast_to(seen, (PROMPT, HD)) > 0) & (row < info_ref[0, 1])
    eye = diagonal((HD, HD))
    for head in range(HEADS_HERE):
        kept, *got = refs[head * GROUP : (head + 1) * GROUP]
        for at in range(QROWS // HD):
            line = jnp.zeros((1, HD), F32)
            for one in got:
                line += one[QROWS + at : QROWS + at + 1, :].astype(F32)
                line += one[QROWS + 4 + at : QROWS + 5 + at, :].astype(F32)
            square = jnp.broadcast_to(line, (HD, HD)) * eye
            spread = jnp.broadcast_to(jnp.sum(square, axis=1, keepdims=True), (HD, HD))
            block = slice(at * HD, (at + 1) * HD)
            numerator = kept[block, :HD]
            for one in got:
                numerator += one[block, :].astype(F32)
            denominator = kept[block, HD:] + spread
            for half in range(HD // PROMPT):
                inner = slice(half * PROMPT, (half + 1) * PROMPT)
                divisor = jnp.where(live, denominator[inner], 1.0)
                result = jnp.where(live, numerator[inner] / divisor, 0.0)
                column = (head * GSIZE + at * 2 + half) * HD
                out_ref[0, :, column : column + HD] = result.astype(BF16)


def finish(info, mask, parts):
    vmem = pl.BlockSpec(memory_space=pltpu.VMEM)
    return pl.pallas_call(
        finish_kernel,
        in_specs=[pl.BlockSpec(memory_space=pltpu.SMEM)] + [vmem] * (1 + len(parts)),
        out_specs=vmem,
        out_shape=jax.ShapeDtypeStruct((1, PROMPT, HEADS_HERE * GSIZE * HD), BF16),
        compiler_params=params(VMEM_ALL),
        cost_estimate=brief(),
        name="finish",
    )(info, mask, *parts)


def add(left, right):
    return (left.astype(F32) + right.astype(F32)).astype(BF16)


def local(
    tile_features,
    projection,
    queries,
    query_gain,
    key_gain,
    tile_count,
    tile_slot,
    cross_mask,
    prompt_length,
):
    own_index = lax.axis_index("dp")
    up_perm = [(i, (i + 1) % NHEAD) for i in range(NHEAD)]
    down_perm = [(i, (i - 1) % NHEAD) for i in range(NHEAD)]
    groups = [list(range(g, g + GROUP)) for g in range(0, lax.axis_size("dp"), GROUP)]
    rows_first = jnp.transpose(tile_features, (1, 0, 2))
    perms = {"uf": up_perm, "ub": up_perm, "df": down_perm, "db": down_perm}
    names = (("uf", "df"), ("ub", "db"))
    running, held, arrived = {}, {}, {}
    later = NHEAD - 1

    def keep_later(start, outs):
        outs = iter(outs)
        for side in range(2):
            for at in range(start, min(2 * start + 1, later)):
                for pair in names:
                    held[pair[side], at] = next(outs)

    def hop(pair):
        for name in pair:
            running[name] = lax.ppermute(running[name], "head", perms[name])

    def last_hop(pair, heads, after=()):
        joined = join_heads(
            heads,
            [running[name] for name in pair],
            [held[name, 1] for name in pair],
            after,
            pair == back,
        )
        for name, one in zip(pair, joined):
            one = lax.ppermute(one, "head", perms[name])
            arrived[name, heads[0]] = one
        return joined

    front, back = names
    *outs, weights = open_ring(projection, rows_first)
    apart = {(name, head): outs[2 * n + head] for n, name in enumerate(front) for head in range(2)}
    parts = ((UP_BACK, BACK, ((0, BACK),)), (DOWN_BACK, BACK, ((0, BACK),)))
    running.update(zip(back, partials(rows_first, weights, parts, 1, 1)))
    whole = (
        (UP_FRONT, HALF, ((0, FRONT), (FRONT, BACK))),
        (DOWN_BACK, HALF, ((BACK, FRONT), (0, BACK))),
    )
    for head in range(HEADS_HERE):
        for name in front:
            apart[name, head] = lax.ppermute(apart[name, head], "head", perms[name])
    low, high = [[apart[name, head] for name in front] for head in range(HEADS_HERE)]
    after = (running["db"], *low)
    keep_later(0, partials(rows_first, weights, whole, 2, 1, after))
    hop(back)
    running.update(zip(front, join_apart(low, high, [held[name, 0] for name in front])))
    for name in back:
        running[name] = add(running[name], held[name, 0])
    after = tuple(running[name] for name in front + back)
    keep_later(1, partials(rows_first, weights, whole, 3, 2, after))
    tile_count, prompt_length, tile_slot, cross_mask, _ = lax.optimization_barrier(
        (tile_count, prompt_length, tile_slot, cross_mask, held["df", 1])
    )
    info = jnp.concatenate([tile_count, prompt_length, tile_slot[0], jnp.zeros((2,), jnp.int32)])
    packed = pack_queries(info[None], cross_mask, queries, held["df", 1])
    packed = lax.all_gather(packed, "dp", axis=0, tiled=True, axis_index_groups=groups)
    for pair in names:
        hop(pair)
    me = jnp.full((1,), own_index, jnp.int32)
    qn, owned = prepare_queries(me, packed, query_gain[None])
    key_line = key_gain[None]
    last = NHEAD - 2

    def parts_of(pair, head):
        up, down = pair
        return arrived[up, head], held[up, last], arrived[down, head], held[down, last]

    def send_back(sent):
        back = []
        for partner in (2, 3, 1):
            pairs = [(i, i ^ partner) for i in range(lax.axis_size("dp"))]
            back.append(lax.ppermute(sent[partner - 1], "dp", pairs))
        return back

    joined = last_hop(front, (0, 2))
    joined = last_hop(back, (0, 1), tuple(joined))
    last_hop(back, (1, 2), (*joined, qn))
    before = front_attention(parts_of(front, 0), qn, key_line)
    final = []
    for head in range(HEADS_HERE):
        kept, *sent = closing_attention(
            head, parts_of(back, head), qn, key_line, before, owned, OVERLAP
        )
        final += [kept] + send_back(sent)
    return finish(info[None], cross_mask, final)


def solution(mesh):
    in_specs = (
        P("dp", None, "head"),
        P("head", None, None),
        P("dp", None, "head"),
        P(),
        P(),
        P("dp"),
        P("dp", None),
        P("dp", None, None),
        P("dp"),
    )
    out_specs = P("dp", None, "head")
    return jax.shard_map(local, mesh=mesh, in_specs=in_specs, out_specs=out_specs, check_vma=False)
```
